256 devices in a mesh: row: 16 (over z_lo, x), col: 16 (over z_hi, y, core).
Axes of the slice: x: 4, y: 4, z: 8 (z_hi: 2, z_lo: 4; z = z_hi * 4 + z_lo), core: 2. Of those that a mesh axis runs over, the one named last changes fastest.
Arguments:
- token_ids: int32 [16, 16, 128], P('row'), may hold values from 0 to 31999
- embedding: bfloat16 [32000, 1024], P(None, 'col'), may hold values from -6 to 6
- up_one: bfloat16 [16, 1024, 4096], P('row', None, 'col'), may hold values from -0.1875 to 0.1875
- down_one: bfloat16 [16, 4096, 1024], P('row', 'col'), may hold values from -0.09375 to 0.09375
- up_two: bfloat16 [16, 1024, 4096], P('col', None, 'row'), may hold values from -0.1875 to 0.1875
- down_two: bfloat16 [16, 4096, 1024], P('col', 'row'), may hold values from -0.09375 to 0.09375
- moment_up_one: bfloat16 [16, 1024, 4096], P('row', None, 'col'), may hold values from -6 to 6
- moment_down_one: bfloat16 [16, 4096, 1024], P('row', 'col'), may hold values from -6 to 6
- moment_up_two: bfloat16 [16, 1024, 4096], P('col', None, 'row'), may hold values from -6 to 6
- moment_down_two: bfloat16 [16, 4096, 1024], P('col', 'row'), may hold values from -6 to 6
- cotangent: bfloat16 [16, 16, 128, 1024], P('row', 'col'), may hold values from -6 to 6
Outputs:
- new_up_one: bfloat16 [16, 1024, 4096], P('row', None, 'col')
- new_down_one: bfloat16 [16, 4096, 1024], P('row', 'col')
- new_up_two: bfloat16 [16, 1024, 4096], P('col', None, 'row')
- new_down_two: bfloat16 [16, 4096, 1024], P('col', 'row')
- new_moment_up_one: bfloat16 [16, 1024, 4096], P('row', None, 'col')
- new_moment_down_one: bfloat16 [16, 4096, 1024], P('row', 'col')
- new_moment_up_two: bfloat16 [16, 1024, 4096], P('col', None, 'row')
- new_moment_down_two: bfloat16 [16, 4096, 1024], P('col', 'row')
The draws below stay inside these ranges and needn't reach their ends.
All inputs are finite; a program needn't handle non-finite values.
Results may differ from the reference program's by a relative error of at most 0.019.
Values may be sent and summed in bfloat16 or wider, within the bound.
A program may use at most 128 MiB of HBM per device.

```python
import jax
import jax.numpy as jnp
from jax import lax

WIDTH = 1024
HIDDEN_SIZE = 4096
VOCAB = 32000
TOK_DEV = 128
GRID_R = 16
GRID_C = 16


def plant(result, rng, low, high):
    dims = result.shape
    index_at = [jax.random.randint(jax.random.fold_in(rng, axis), (), 0, dims[axis]) for axis in range(len(dims))]
    result = result.at[tuple(index_at)].set(low)
    longest = dims.index(max(dims))
    index_at[longest] = (index_at[longest] + 1) % dims[longest]
    return result.at[tuple(index_at)].set(high)


def steps_of(own_key, shape, cuts, least, largest):
    gain, own = 1.0, jax.random.fold_in(own_key, 6)
    for dim, blocks in cuts:
        draws = jnp.exp(jax.random.uniform(jax.random.fold_in(own, dim), (blocks,), jnp.float32, least / len(cuts), largest / len(cuts)))
        gain = gain * jnp.repeat(draws, shape[dim] // blocks).reshape([-1 if axis == dim else 1 for axis in range(len(shape))])
    return gain


def centred(stream_key, dims, spread, most, cuts=(), held_as=jnp.bfloat16):
    level = steps_of(stream_key, dims, cuts, -0.22, 0.18) if cuts else 1.0
    result = jax.random.normal(stream_key, dims, jnp.float32) * spread * level
    return jnp.minimum(jnp.maximum(result, -most), most).astype(held_as)


def setup_inputs(seed: int = 0) -> dict:
    keys = jax.random.split(jax.random.key(seed), 12)
    token_ids = plant(jax.random.randint(keys[0], (GRID_R, GRID_C, TOK_DEV), 0, VOCAB), jax.random.fold_in(keys[0], 1), 0, VOCAB - 1).astype(jnp.int32)
    embedding = centred(keys[1], (VOCAB, WIDTH), 1.0, 6.0, ((1, 16),))
    up_one = centred(keys[2], (GRID_R, WIDTH, HIDDEN_SIZE), WIDTH ** -0.5, 0.1875, ((0, 16), (2, 16)))
    down_one = centred(keys[3], (GRID_R, HIDDEN_SIZE, WIDTH), HIDDEN_SIZE ** -0.5, 0.09375, ((0, 16), (1, 16)))
    up_two = centred(keys[4], (GRID_C, WIDTH, HIDDEN_SIZE), WIDTH ** -0.5, 0.1875, ((0, 16), (2, 16)))
    down_two = centred(keys[5], (GRID_C, HIDDEN_SIZE, WIDTH), HIDDEN_SIZE ** -0.5, 0.09375, ((0, 16), (1, 16)))
    moment_up_one = centred(keys[6], (GRID_R, WIDTH, HIDDEN_SIZE), 1.0, 6.0, ((0, 16), (2, 16)))
    moment_down_one = centred(keys[7], (GRID_R, HIDDEN_SIZE, WIDTH), 1.0, 6.0, ((0, 16), (1, 16)))
    moment_up_two = centred(keys[8], (GRID_C, WIDTH, HIDDEN_SIZE), 1.0, 6.0, ((0, 16), (2, 16)))
    moment_down_two = centred(keys[9], (GRID_C, HIDDEN_SIZE, WIDTH), 1.0, 6.0, ((0, 16), (1, 16)))
    cotangent = centred(keys[10], (GRID_R, GRID_C, TOK_DEV, WIDTH), 1.0, 6.0, ((0, 16), (1, 16)))
    return {"token_ids": token_ids, "embedding": embedding, "up_one": up_one, "down_one": down_one, "up_two": up_two, "down_two": down_two, "moment_up_one": moment_up_one, "moment_down_one": moment_down_one, "moment_up_two": moment_up_two, "moment_down_two": moment_down_two, "cotangent": cotangent}


epsilon = 1e-06
momentum_decay = 0.9
outer_rate = 0.7
inner_rate = 0.01

def normalize(values):
    factor = lax.rsqrt(lax.optimization_barrier(jnp.mean(values * values, axis=-1, keepdims=True)) + epsilon)
    return values * factor

def normalize_back(values, upstream):
    factor = lax.rsqrt(lax.optimization_barrier(jnp.mean(values * values, axis=-1, keepdims=True)) + epsilon)
    return factor * upstream - values * (factor * factor * factor) * lax.optimization_barrier(jnp.mean(upstream * values, axis=-1, keepdims=True))

def activation(values):
    return jax.nn.gelu(values, approximate=True)

def activation_slope(values, upstream):
    return jax.vjp(activation, values)[1](upstream)[0]

def contract_rows(first_operand, second_operand):
    return lax.dot_general(first_operand, second_operand, (((0,), (0,)), ((), ())), preferred_element_type=jnp.float32)

def contract_cols(first_operand, second_operand):
    return lax.dot_general(first_operand, second_operand, (((1,), (1,)), ((), ())), preferred_element_type=jnp.float32)

def blocked_sum(operand, weights, blocks):
    height = operand.shape[0]
    inner = operand.shape[1] // blocks
    pieces = operand.reshape(height, blocks, inner).astype(jnp.float32)
    stacked = weights.reshape(blocks, inner, weights.shape[1]).astype(jnp.float32)
    terms = jnp.einsum('mkb,kbd->kmd', pieces, stacked)
    rounded = lax.optimization_barrier(terms.astype(jnp.bfloat16))
    return lax.optimization_barrier(jnp.sum(rounded.astype(jnp.float32), axis=0))

def outer_update(parameter, moment, gradient, sharers):
    average = gradient / sharers
    new_moment = momentum_decay * moment.astype(jnp.float32) + average
    new_parameter = parameter.astype(jnp.float32) - outer_rate * inner_rate * (average + momentum_decay * new_moment)
    return (new_parameter.astype(jnp.bfloat16), new_moment.astype(jnp.bfloat16))

def level_one_forward(embedding, ids_group, up_weight, down_weight):
    inputs = jnp.take(embedding, ids_group.reshape(-1), axis=0)
    normed = normalize(inputs.astype(jnp.float32)).astype(jnp.bfloat16)
    pre_act = jnp.dot(normed, up_weight, preferred_element_type=jnp.float32)
    hidden = activation(pre_act).astype(jnp.bfloat16)
    middle = inputs.astype(jnp.float32) + blocked_sum(hidden, down_weight, GRID_C)
    return (normed, pre_act, hidden, middle)

def reference(token_ids, embedding, up_one, down_one, up_two, down_two, moment_up_one, moment_down_one, moment_up_two, moment_down_two, cotangent):

    def first_pass(packed):
        ids_group, up_weight, down_weight = packed
        middle = level_one_forward(embedding, ids_group, up_weight, down_weight)[3]
        return middle.reshape(GRID_C, TOK_DEV, WIDTH)
    middles = lax.map(first_pass, (token_ids, up_one, down_one))

    def second_pass(packed):
        middle_col, cot_col, up_weight, down_weight, moment_up, moment_down = packed
        values = middle_col.reshape(GRID_R * TOK_DEV, WIDTH)
        upstream = cot_col.reshape(GRID_R * TOK_DEV, WIDTH)
        normed = normalize(values).astype(jnp.bfloat16)
        pre_act = jnp.dot(normed, up_weight, preferred_element_type=jnp.float32)
        hidden = activation(pre_act).astype(jnp.bfloat16)
        grad_down = contract_rows(hidden, upstream)
        back_hidden = contract_cols(upstream, down_weight)
        slope = activation_slope(pre_act, back_hidden).astype(jnp.bfloat16)
        grad_up = contract_rows(normed, slope)
        back_normed = blocked_sum(slope, up_weight.T, GRID_R)
        back_middle = (upstream.astype(jnp.float32) + normalize_back(values, back_normed)).astype(jnp.bfloat16)
        new_up, new_moment_up = outer_update(up_weight, moment_up, grad_up, GRID_R)
        new_down, new_moment_down = outer_update(down_weight, moment_down, grad_down, GRID_R)
        return (back_middle.reshape(GRID_R, TOK_DEV, WIDTH), new_up, new_down, new_moment_up, new_moment_down)
    second = lax.map(second_pass, (jnp.swapaxes(middles, 0, 1), jnp.swapaxes(cotangent, 0, 1), up_two, down_two, moment_up_two, moment_down_two))
    back_middles = jnp.swapaxes(second[0], 0, 1)

    def third_pass(packed):
        ids_group, up_weight, down_weight, moment_up, moment_down, back_group = packed
        normed, pre_act, hidden, middle = level_one_forward(embedding, ids_group, up_weight, down_weight)
        upstream = back_group.reshape(GRID_C * TOK_DEV, WIDTH)
        grad_down = contract_rows(hidden, upstream)
        back_hidden = contract_cols(upstream, down_weight)
        slope = activation_slope(pre_act, back_hidden).astype(jnp.bfloat16)
        grad_up = contract_rows(normed, slope)
        new_up, new_moment_up = outer_update(up_weight, moment_up, grad_up, GRID_C)
        new_down, new_moment_down = outer_update(down_weight, moment_down, grad_down, GRID_C)
        return (new_up, new_down, new_moment_up, new_moment_down)
    third = lax.map(third_pass, (token_ids, up_one, down_one, moment_up_one, moment_down_one, back_middles))
    return (third[0], third[1], second[1], second[2], third[2], third[3], second[3], second[4])
```

```python
import functools

import jax
import jax.numpy as jnp
from jax import lax
from jax.experimental import pallas as pl
from jax.experimental.pallas import tpu as pltpu
from jax.sharding import PartitionSpec as P

epsilon = 1e-06
momentum_decay = 0.9
outer_rate = 0.7
inner_rate = 0.01
MESH = pl.DeviceIdType.MESH
RING = 4
TOK = 128


def activation(values):
    return jax.nn.gelu(values, approximate=True)


def activation_slope(values, upstream):
    return jax.vjp(activation, values)[1](upstream)[0]


def contract_rows(first_operand, second_operand):
    return lax.dot_general(
        first_operand, second_operand, (((0,), (0,)), ((), ())), preferred_element_type=jnp.float32
    )


def contract_cols(first_operand, second_operand):
    return lax.dot_general(
        first_operand, second_operand, (((1,), (1,)), ((), ())), preferred_element_type=jnp.float32
    )


def outer_update(parameter, moment, gradient, sharers):
    average = gradient / sharers
    new_moment = momentum_decay * moment.astype(jnp.float32) + average
    new_parameter = parameter.astype(jnp.float32) - outer_rate * inner_rate * (
        average + momentum_decay * new_moment
    )
    return (new_parameter.astype(jnp.bfloat16)[None], new_moment.astype(jnp.bfloat16)[None])


class Place:
    def __init__(self):
        row, col = lax.axis_index("row"), lax.axis_index("col")
        self.zl, self.x = row // 4, row % 4
        self.zh, self.y, self.k = col // 8, (col // 2) % 4, col % 2
        self.stay = (self.zl // 2) == self.k
        other_zl = (self.zl + 2) % 4
        self.swap = (other_zl * 4 + self.x, self.zh * 8 + self.y * 2 + (1 - self.k))


class ColGroup:
    def __init__(self, place):
        self.place = place
        self.p, self.t, self.k = place.zh, place.y, place.k

    def device(self, p, t, k):
        return (self.place.zl * 4 + self.place.x, p * 8 + t * 2 + k)

    @staticmethod
    def slot(p, t, k):
        return p * 8 + t * 2 + k


class RowGroup:
    def __init__(self, place):
        self.place = place
        self.p, self.t, self.k = place.zl % 2, place.x, place.k
        self.half = place.zl // 2

    def device(self, p, t, k):
        return ((self.half * 2 + p) * 4 + t, self.place.zh * 8 + self.place.y * 2 + k)

    @staticmethod
    def slot(p, t, k):
        return (2 * k + p) * 4 + t


def near(group):
    p, t, k = group.p, group.t, group.k
    up, down = (t + 1) % RING, (t + RING - 1) % RING
    return {
        "pair": group.device(1 - p, t, k),
        "sibling": group.device(p, t, 1 - k),
        "up": group.device(p, up, k),
        "down": group.device(p, down, k),
    }


def greet(devices):
    barrier = pltpu.get_barrier_semaphore()
    for device in devices:
        pl.semaphore_signal(barrier, inc=1, device_id=device, device_id_type=MESH)
    pl.semaphore_wait(barrier, len(devices))


class Mail:
    def __init__(self, send_sem, recv_sem):
        self.send_sem, self.recv_sem = send_sem, recv_sem
        self.sent = []

    def copy(self, number, src, dst, device):
        return pltpu.make_async_remote_copy(
            src_ref=src,
            dst_ref=dst,
            send_sem=self.send_sem.at[number],
            recv_sem=self.recv_sem.at[number],
            device_id=device,
            device_id_type=MESH,
        )

    def send(self, number, src, dst, device):
        copy = self.copy(number, src, dst, device)
        copy.start()
        self.sent.append(copy)

    def arrived(self, number, ref, device):
        self.copy(number, ref, ref, device).wait_recv()

    def finish(self):
        for copy in self.sent:
            copy.wait_send()
        self.sent = []


GATHER_MESSAGES = 17


class Gather:
    def __init__(self, group, mail, base, region, half):
        self.g, self.mail, self.base, self.region, self.half = group, mail, base, region, half
        self.peers = near(group)

    def send(self, m, ref, to):
        self.mail.send(self.base + m, ref, ref, self.peers[to])

    def got(self, m, ref):
        self.mail.arrived(self.base + m, ref, self.peers["sibling"])

    def start(self):
        g = self.g
        own = self.region(g.p, g.t, g.k)
        self.send(0, own, "pair")
        self.send(2, own, "up")
        self.send(3, own, "down")
        self.send(1, own, "sibling")

    def pair_arrived(self):
        g = self.g
        q = 1 - g.p
        ref = self.region(q, g.t, g.k)
        self.got(0, ref)
        self.send(4, ref, "up")
        self.send(5, ref, "down")
        self.send(6, ref, "sibling")

    def ring_arrived(self, which):
        g = self.g
        q, first, fwd = ((g.p, 2, 7), (1 - g.p, 4, 11))[which]
        before, after = (g.t + RING - 1) % RING, (g.t + 1) % RING
        ref = self.region(q, before, g.k)
        self.got(first, ref)
        self.send(fwd, self.half(q, before, g.k, 0), "up")
        self.send(fwd + 1, ref, "sibling")
        ref = self.region(q, after, g.k)
        self.got(first + 1, ref)
        self.send(fwd + 2, self.half(q, after, g.k, 1), "down")
        self.send(fwd + 3, ref, "sibling")

    def far_arrived(self, which):
        g = self.g
        q, fwd, last = ((g.p, 7, 15), (1 - g.p, 11, 16))[which]
        far = (g.t + 2) % RING
        self.got(fwd, self.half(q, far, g.k, 0))
        self.got(fwd + 2, self.half(q, far, g.k, 1))
        self.send(last, self.region(q, far, g.k), "sibling")

    def sibling_arrived(self):
        g = self.g
        before, after, far = (g.t + RING - 1) % RING, (g.t + 1) % RING, (g.t + 2) % RING
        o = 1 - g.k
        for m, q, t in (
            (1, g.p, g.t),
            (6, 1 - g.p, g.t),
            (8, g.p, before),
            (10, g.p, after),
            (12, 1 - g.p, before),
            (14, 1 - g.p, after),
            (15, g.p, far),
            (16, 1 - g.p, far),
        ):
            self.got(m, self.region(q, t, o))

    def run(self):
        self.start()
        self.pair_arrived()
        self.ring_arrived(0)
        self.ring_arrived(1)
        self.far_arrived(0)
        self.far_arrived(1)
        self.sibling_arrived()


SCATTER_MESSAGES = 8 + 4 + 8 + 1


def scatter_sum(group, mail, base, part, from_sibling, sums, from_far, from_near, from_pair):
    f32, b16 = jnp.float32, jnp.bfloat16
    p, t, k = group.p, group.t, group.k
    peers = near(group)
    up, down, far = (t + 1) % RING, (t + RING - 1) % RING, (t + 2) % RING
    top, low = pl.ds(0, TOK // 2), pl.ds(TOK // 2, TOK // 2)
    order = [(q, s) for q in (1, 0) for s in (2, 1, 3, 0)]

    def place(q, s):
        return (1 - p if q else p), (t + s) % RING

    def cell(q, s):
        return q * 4 + s

    for q, s in order:
        side, at = place(q, s)
        mail.send(
            base + cell(q, s),
            part.at[group.slot(side, at, 1 - k)],
            from_sibling.at[cell(q, s)],
            peers["sibling"],
        )

    def pair_sum(q, s):
        side, at = place(q, s)
        mail.arrived(base + cell(q, s), from_sibling.at[cell(q, s)], peers["sibling"])
        sums[cell(q, s)] = (
            part[group.slot(side, at, k)].astype(f32) + from_sibling[cell(q, s)].astype(f32)
        ).astype(b16)

    far_base, near_base, pair_base = base + 8, base + 12, base + 20
    for q in (1, 0):
        pair_sum(q, 2)
        mail.send(far_base + 2 * q, sums.at[cell(q, 2), top], from_far.at[2 * q], peers["up"])
        mail.send(far_base + 2 * q + 1, sums.at[cell(q, 2), low], from_far.at[2 * q + 1], peers["down"])
        pair_sum(q, 1)
        mail.send(near_base + 4 * q, sums.at[cell(q, 1), low], from_near.at[2 * q, low], peers["up"])
        pair_sum(q, 3)
        mail.send(near_base + 4 * q + 1, sums.at[cell(q, 3), top], from_near.at[2 * q + 1, top], peers["down"])
        pair_sum(q, 0)
    for q in (1, 0):
        mail.arrived(far_base + 2 * q, from_far.at[2 * q], peers["sibling"])
        sums[cell(q, 1), top] = (
            sums[cell(q, 1), top].astype(f32) + from_far[2 * q].astype(f32)
        ).astype(b16)
        mail.send(near_base + 4 * q + 2, sums.at[cell(q, 1), top], from_near.at[2 * q, top], peers["up"])
        mail.arrived(far_base + 2 * q + 1, from_far.at[2 * q + 1], peers["sibling"])
        sums[cell(q, 3), low] = (
            sums[cell(q, 3), low].astype(f32) + from_far[2 * q + 1].astype(f32)
        ).astype(b16)
        mail.send(near_base + 4 * q + 3, sums.at[cell(q, 3), low], from_near.at[2 * q + 1, low], peers["down"])

    def total(q):
        mail.arrived(near_base + 4 * q, from_near.at[2 * q, low], peers["sibling"])
        mail.arrived(near_base + 4 * q + 1, from_near.at[2 * q + 1, top], peers["sibling"])
        mail.arrived(near_base + 4 * q + 2, from_near.at[2 * q, top], peers["sibling"])
        mail.arrived(near_base + 4 * q + 3, from_near.at[2 * q + 1, low], peers["sibling"])
        return (
            sums[cell(q, 0)].astype(f32)
            + from_near[2 * q].astype(f32)
            + from_near[2 * q + 1].astype(f32)
        )

    sums[cell(1, 0)] = total(1).astype(b16)
    mail.send(pair_base, sums.at[cell(1, 0)], from_pair, peers["pair"])
    mine = total(0)
    mail.arrived(pair_base, from_pair, peers["sibling"])
    return mine + from_pair[...].astype(f32)


def scatter_scratch(width):
    b16 = jnp.bfloat16
    return [
        pltpu.VMEM((8, TOK, width), b16),
        pltpu.VMEM((8, TOK, width), b16),
        pltpu.VMEM((4, TOK // 2, width), b16),
        pltpu.VMEM((4, TOK, width), b16),
        pltpu.VMEM((TOK, width), b16),
    ]


def token_regions(buf, slot):
    def region(p, t, k):
        return buf.at[slot(p, t, k)]

    def half(p, t, k, h):
        return buf.at[slot(p, t, k), pl.ds(h * (TOK // 2), TOK // 2)]

    return region, half


def swap_or_keep(place, mail, number, src, dst):
    @pl.when(place.stay)
    def _():
        dst[...] = src[...]

    @pl.when(jnp.logical_not(place.stay))
    def _():
        mail.copy(number, src, dst, place.swap).start()


def swap_wait(place, mail, number, src, dst):
    @pl.when(jnp.logical_not(place.stay))
    def _():
        mail.copy(number, src, dst, place.swap).wait()


def first_kernel(
    pieces, cot, up_two, down_two, inputs, cots, up_out, down_out, wide, other, send_sem, recv_sem
):
    place = Place()
    col, row = ColGroup(place), RowGroup(place)
    mail = Mail(send_sem, recv_sem)
    peers_c, peers_r = near(col), near(row)
    greet(
        [peers_c["sibling"], peers_c["pair"], peers_c["up"], peers_c["down"]]
        + [peers_r["pair"], peers_r["up"], peers_r["down"], place.swap]
    )
    k = place.k
    rows = pieces.shape[0] // 2
    own = pieces[...]
    wide[...] = jnp.concatenate([own, own], axis=1)
    mail.send(0, wide.at[pl.ds((1 - k) * rows, rows)], other, peers_c["sibling"])
    slot = row.slot(row.p, row.t, row.k)
    swap_slot = row.slot(row.p, row.t, 1 - row.k)

    @pl.when(place.stay)
    def _():
        cots[slot] = cot[...]

    @pl.when(jnp.logical_not(place.stay))
    def _():
        mail.copy(1, cot, cots.at[swap_slot], place.swap).start()

    mail.arrived(0, other, peers_c["sibling"])
    lane = lax.broadcasted_iota(jnp.int32, (rows, 128), 1) // 64
    here = pl.ds(pl.multiple_of((place.zh * 4 + place.y) * 128, 128), 128)
    inputs[pl.ds(k * rows, rows), here] = jnp.where(
        lane == k, wide[pl.ds(k * rows, rows)], other[...]
    )

    def region(p, t, k):
        return inputs.at[pl.ds(k * rows, rows), pl.ds(pl.multiple_of((p * 4 + t) * 128, 128), 128)]

    def half(p, t, k, h):
        return inputs.at[
            pl.ds(k * rows + h * (rows // 2), rows // 2),
            pl.ds(pl.multiple_of((p * 4 + t) * 128, 128), 128),
        ]

    tokens = Gather(col, mail, 4, region, half)
    tokens.start()
    swap_wait(place, mail, 1, cot, cots.at[swap_slot])
    upstream = Gather(row, mail, 4 + GATHER_MESSAGES, *token_regions(cots, row.slot))
    upstream.start()
    swap_or_keep(place, mail, 2, up_two, up_out)
    swap_or_keep(place, mail, 3, down_two, down_out)
    for gather in (tokens, upstream):
        gather.pair_arrived()
    for which in (0, 1):
        for gather in (tokens, upstream):
            gather.ring_arrived(which)
    for which in (0, 1):
        for gather in (tokens, upstream):
            gather.far_arrived(which)
    for gather in (tokens, upstream):
        gather.sibling_arrived()
    swap_wait(place, mail, 2, up_two, up_out)
    swap_wait(place, mail, 3, down_two, down_out)
    mail.finish()


def second_kernel(part, own_input, middle, normed, mine, *scratch):
    *scatter, send_sem, recv_sem = scratch
    place = Place()
    col, row = ColGroup(place), RowGroup(place)
    mail = Mail(send_sem, recv_sem)
    peers_c, peers_r = near(col), near(row)
    greet(
        [peers_c["sibling"], peers_c["pair"], peers_c["up"], peers_c["down"]]
        + [peers_r["pair"], peers_r["up"], peers_r["down"], place.swap]
    )
    mixed = scatter_sum(col, mail, 1, part, *scatter)
    values = own_input[...].astype(jnp.float32) + mixed
    middle[...] = values
    factor = lax.rsqrt(jnp.mean(values * values, axis=-1, keepdims=True) + epsilon)
    mine[...] = (values * factor).astype(jnp.bfloat16)
    slot = row.slot(row.p, row.t, row.k)
    swap_slot = row.slot(row.p, row.t, 1 - row.k)

    @pl.when(place.stay)
    def _():
        normed[slot] = mine[...]

    @pl.when(jnp.logical_not(place.stay))
    def _():
        mail.copy(0, mine, normed.at[swap_slot], place.swap).start()

    swap_wait(place, mail, 0, mine, normed.at[swap_slot])
    Gather(row, mail, 1 + SCATTER_MESSAGES, *token_regions(normed, row.slot)).run()
    mail.finish()


def third_kernel(
    part, middle, cot, grad_up, grad_down, group, grad_up_out, grad_down_out, mine, back, *scratch
):
    *scatter, send_sem, recv_sem = scratch
    place = Place()
    col, row = ColGroup(place), RowGroup(place)
    mail = Mail(send_sem, recv_sem)
    peers_c, peers_r = near(col), near(row)
    greet(
        [peers_c["sibling"], peers_c["pair"], peers_c["up"], peers_c["down"]]
        + [peers_r["pair"], peers_r["up"], peers_r["down"], place.swap]
    )
    mine[...] = scatter_sum(row, mail, 3, part, *scatter).astype(jnp.bfloat16)
    swap_or_keep(place, mail, 0, mine, back)
    swap_wait(place, mail, 0, mine, back)
    swap_or_keep(place, mail, 1, grad_up, grad_up_out)
    swap_or_keep(place, mail, 2, grad_down, grad_down_out)
    upstream = back[...].astype(jnp.float32)
    values = middle[...]
    factor = lax.rsqrt(jnp.mean(values * values, axis=-1, keepdims=True) + epsilon)
    through = factor * upstream - values * (factor * factor * factor) * jnp.mean(
        upstream * values, axis=-1, keepdims=True
    )
    group[col.slot(col.p, col.t, col.k)] = (cot[...].astype(jnp.float32) + through).astype(
        jnp.bfloat16
    )
    Gather(col, mail, 3 + SCATTER_MESSAGES, *token_regions(group, col.slot)).run()
    swap_wait(place, mail, 1, grad_up, grad_up_out)
    swap_wait(place, mail, 2, grad_down, grad_down_out)
    mail.finish()


def call(kernel, name, out_shape, args, scratch, messages, number):
    vmem = pl.BlockSpec(memory_space=pltpu.VMEM)
    return pl.pallas_call(
        kernel,
        name=name,
        out_shape=out_shape,
        in_specs=[vmem] * len(args),
        out_specs=[vmem] * len(out_shape),
        scratch_shapes=scratch
        + [pltpu.SemaphoreType.DMA((messages,)), pltpu.SemaphoreType.DMA((messages,))],
        compiler_params=pltpu.CompilerParams(
            collective_id=number, has_side_effects=True, vmem_limit_bytes=48 * 2**20
        ),
    )(*args)


def on_device(
    token_ids,
    embedding,
    up_one,
    down_one,
    up_two,
    down_two,
    moment_up_one,
    moment_down_one,
    moment_up_two,
    moment_down_two,
    cotangent,
):
    b16, f32 = jnp.bfloat16, jnp.float32
    sharers = 16
    col_place = lax.axis_index("col")
    width = cotangent.shape[3]
    own_cot = cotangent[0, 0]
    ids_flat = token_ids[0].reshape(-1)
    tokens = ids_flat.shape[0]
    pieces = embedding.at[ids_flat].get(mode="promise_in_bounds")
    whole = jax.ShapeDtypeStruct((16, TOK, width), b16)
    inputs, cots, up_home, down_home = call(
        first_kernel,
        "first",
        [
            jax.ShapeDtypeStruct((tokens, width), b16),
            whole,
            jax.ShapeDtypeStruct(up_two.shape[1:], b16),
            jax.ShapeDtypeStruct(down_two.shape[1:], b16),
        ],
        [pieces, own_cot, up_two[0], down_two[0]],
        [pltpu.VMEM((tokens, 128), b16), pltpu.VMEM((tokens // 2, 128), b16)],
        4 + 2 * GATHER_MESSAGES,
        0,
    )
    wide = inputs.astype(f32)
    factor = lax.rsqrt(jnp.mean(wide * wide, axis=-1, keepdims=True) + epsilon)
    normed_one = (wide * factor).astype(b16)
    pre_one = jnp.dot(normed_one, up_one[0], preferred_element_type=f32)
    act_one = activation(pre_one).astype(b16)
    part_one = jnp.dot(act_one, down_one[0], preferred_element_type=f32).astype(b16)
    own_input = lax.dynamic_slice_in_dim(inputs, col_place * TOK, TOK, 0)
    middle, normed_two = call(
        second_kernel,
        "second",
        [jax.ShapeDtypeStruct((TOK, width), f32), whole],
        [part_one.reshape(16, TOK, width), own_input],
        [pltpu.VMEM((TOK, width), b16)] + scatter_scratch(width),
        1 + SCATTER_MESSAGES + GATHER_MESSAGES,
        1,
    )
    normed_two = normed_two.reshape(tokens, width)
    cot_rows = cots.reshape(tokens, width)
    pre_two = jnp.dot(normed_two, up_home, preferred_element_type=f32)
    act_two = activation(pre_two).astype(b16)
    grad_down_two = contract_rows(act_two, cot_rows).astype(b16)
    back_two = contract_cols(cot_rows, down_home)
    slope_two = activation_slope(pre_two, back_two).astype(b16)
    grad_up_two = contract_rows(normed_two, slope_two).astype(b16)
    part_two = contract_cols(slope_two, up_home).astype(b16)
    group, grad_up_two, grad_down_two = call(
        third_kernel,
        "third",
        [
            whole,
            jax.ShapeDtypeStruct(up_two.shape[1:], b16),
            jax.ShapeDtypeStruct(down_two.shape[1:], b16),
        ],
        [part_two.reshape(16, TOK, width), middle, own_cot, grad_up_two, grad_down_two],
        [pltpu.VMEM((TOK, width), b16)] * 2 + scatter_scratch(width),
        3 + SCATTER_MESSAGES + GATHER_MESSAGES,
        2,
    )
    group = group.reshape(tokens, width)
    grad_down_one = contract_rows(act_one, group)
    back_one = contract_cols(group, down_one[0])
    slope_one = activation_slope(pre_one, back_one).astype(b16)
    grad_up_one = contract_rows(normed_one, slope_one)
    new_up_one, new_moment_up_one = outer_update(up_one[0], moment_up_one[0], grad_up_one, sharers)
    new_down_one, new_moment_down_one = outer_update(
        down_one[0], moment_down_one[0], grad_down_one, sharers
    )
    new_up_two, new_moment_up_two = outer_update(
        up_two[0], moment_up_two[0], grad_up_two.astype(f32), sharers
    )
    new_down_two, new_moment_down_two = outer_update(
        down_two[0], moment_down_two[0], grad_down_two.astype(f32), sharers
    )
    return (
        new_up_one,
        new_down_one,
        new_up_two,
        new_down_two,
        new_moment_up_one,
        new_moment_down_one,
        new_moment_up_two,
        new_moment_down_two,
    )


def solution(mesh):
    in_specs = (
        P("row", None, None),
        P(None, "col"),
        P("row", None, "col"),
        P("row", "col", None),
        P("col", None, "row"),
        P("col", "row", None),
        P("row", None, "col"),
        P("row", "col", None),
        P("col", None, "row"),
        P("col", "row", None),
        P("row", "col", None, None),
    )
    out_specs = (
        P("row", None, "col"),
        P("row", "col", None),
        P("col", None, "row"),
        P("col", "row", None),
        P("row", None, "col"),
        P("row", "col", None),
        P("col", None, "row"),
        P("col", "row", None),
    )
    return jax.shard_map(
        on_device, mesh=mesh, in_specs=in_specs, out_specs=out_specs, check_vma=False
    )
```

```python
import functools

import jax
import jax.numpy as jnp
from jax import lax
from jax.experimental import pallas as pl
from jax.experimental.pallas import tpu as pltpu
from jax.sharding import PartitionSpec as P

epsilon = 1e-06
momentum_decay = 0.9
outer_rate = 0.7
inner_rate = 0.01
MESH = pl.DeviceIdType.MESH
RING = 4
PATHS = 16
TOKENS = 128
GROUPS = 2
PART = TOKENS // GROUPS
ROWS = PATHS * PART
LAG = 9
CHUNK = 256
f32, b16 = jnp.float32, jnp.bfloat16


def outer_update(parameter, moment, gradient, sharers):
    average = gradient / sharers
    new_moment = momentum_decay * moment.astype(f32) + average
    new_parameter = parameter.astype(f32) - outer_rate * inner_rate * (
        average + momentum_decay * new_moment
    )
    return (new_parameter.astype(b16)[None], new_moment.astype(b16)[None])


def gelu_and_slope(v):
    scale, cubic = 0.7978845608028654, 0.044715
    square = v * v
    t = jnp.tanh(scale * v * (1.0 + cubic * square))
    half = 0.5 * (1.0 + t)
    slope = half + 0.5 * v * (1.0 - t * t) * (scale * (1.0 + 3.0 * cubic * square))
    return v * half, slope


def dot(a, b):
    return jnp.dot(a, b, preferred_element_type=f32)


def dot_rows(a, b):
    return lax.dot_general(a, b, (((0,), (0,)), ((), ())), preferred_element_type=f32)


def dot_cols(a, b):
    return lax.dot_general(a, b, (((1,), (1,)), ((), ())), preferred_element_type=f32)


class Place:
    def __init__(self):
        row, col = lax.axis_index("row"), lax.axis_index("col")
        self.zl, self.x = row // 4, row % 4
        self.zh, self.y, self.k = col // 8, (col // 2) % 4, col % 2
        self.stay = (self.zl // 2) == self.k
        other_zl = (self.zl + 2) % 4
        self.swap = (other_zl * 4 + self.x, self.zh * 8 + self.y * 2 + (1 - self.k))


class ColGroup:
    def __init__(self, place):
        self.place = place
        self.p, self.t, self.k = place.zh, place.y, place.k

    def device(self, p, t, k):
        return (self.place.zl * 4 + self.place.x, p * 8 + t * 2 + k)


class RowGroup:
    def __init__(self, place):
        self.place = place
        self.p, self.t, self.k = place.zl % 2, place.x, place.k
        self.half = place.zl // 2

    def device(self, p, t, k):
        return ((self.half * 2 + p) * 4 + t, self.place.zh * 8 + self.place.y * 2 + k)


def slot(p, t, k):
    return k * 8 + p * 4 + t


def first_row(g, p, t, k):
    return pl.multiple_of((g * PATHS + slot(p, t, k)) * PART, PART)


def near(group):
    p, t, k = group.p, group.t, group.k
    up, down = (t + 1) % RING, (t + RING - 1) % RING
    return {
        "pair": group.device(1 - p, t, k),
        "sibling": group.device(p, t, 1 - k),
        "up": group.device(p, up, k),
        "down": group.device(p, down, k),
    }


def greet(devices):
    barrier = pltpu.get_barrier_semaphore()
    for device in devices:
        pl.semaphore_signal(barrier, inc=1, device_id=device, device_id_type=MESH)
    pl.semaphore_wait(barrier, len(devices))


class Mail:
    def __init__(self, send_sem, recv_sem):
        self.send_sem, self.recv_sem = send_sem, recv_sem
        self.sent = []
        self.used = 0

    def take(self, count):
        self.used += count
        return self.used - count

    def copy(self, number, src, dst, device):
        return pltpu.make_async_remote_copy(
            src_ref=src,
            dst_ref=dst,
            send_sem=self.send_sem.at[number],
            recv_sem=self.recv_sem.at[number],
            device_id=device,
            device_id_type=MESH,
        )

    def send(self, number, src, dst, device):
        copy = self.copy(number, src, dst, device)
        copy.start()
        self.sent.append(copy)

    def arrived(self, number, ref, device):
        self.copy(number, ref, ref, device).wait_recv()

    def finish(self):
        for copy in self.sent:
            copy.wait_send()
        self.sent = []


class Gather:
    def __init__(self, group, mail, region, half):
        self.g, self.mail, self.region, self.half = group, mail, region, half
        self.base = mail.take(17)
        self.peers = near(group)

    def send(self, m, ref, to):
        self.mail.send(self.base + m, ref, ref, self.peers[to])

    def got(self, m, ref):
        self.mail.arrived(self.base + m, ref, self.peers["sibling"])

    def steps(self):
        g = self.g
        p, t, k = g.p, g.t, g.k
        before, after, far = (t + RING - 1) % RING, (t + 1) % RING, (t + 2) % RING
        own = self.region(p, t, k)
        self.send(0, own, "pair")
        self.send(2, own, "up")
        self.send(3, own, "down")
        self.send(1, own, "sibling")
        yield
        for q, first, fwd in ((p, 2, 7), (1 - p, 4, 11)):
            if first == 4:
                ref = self.region(q, t, k)
                self.got(0, ref)
                self.send(4, ref, "up")
                self.send(5, ref, "down")
                self.send(6, ref, "sibling")
                yield
            ref = self.region(q, before, k)
            self.got(first, ref)
            self.send(fwd, self.half(q, before, k, 0), "up")
            self.send(fwd + 1, ref, "sibling")
            ref = self.region(q, after, k)
            self.got(first + 1, ref)
            self.send(fwd + 2, self.half(q, after, k, 1), "down")
            self.send(fwd + 3, ref, "sibling")
            yield
        for q, fwd, last in ((p, 7, 15), (1 - p, 11, 16)):
            self.got(fwd, self.half(q, far, k, 0))
            self.got(fwd + 2, self.half(q, far, k, 1))
            self.send(last, self.region(q, far, k), "sibling")
            yield
        for m, q, s in (
            (1, p, t),
            (6, 1 - p, t),
            (8, p, before),
            (10, p, after),
            (12, 1 - p, before),
            (14, 1 - p, after),
            (15, p, far),
            (16, 1 - p, far),
        ):
            self.got(m, self.region(q, s, 1 - k))


def token_regions(buf, g):
    def region(p, t, k):
        return buf.at[pl.ds(first_row(g, p, t, k), PART)]

    def half(p, t, k, h):
        return buf.at[pl.ds(first_row(g, p, t, k) + h * (PART // 2), PART // 2)]

    return region, half


def add_rows(dst, at, left, left_at, right, right_at, count):
    step = 16

    def body(i, _):
        off = i * step
        dst[pl.ds(at + off, step)] = (
            left[pl.ds(left_at + off, step)].astype(f32)
            + right[pl.ds(right_at + off, step)].astype(f32)
        ).astype(b16)
        return 0

    lax.fori_loop(0, count // step, body, 0, unroll=2)


class Scatter:
    def __init__(self, group, mail, g, part, bufs, out):
        self.g, self.mail, self.n, self.part, self.out = group, mail, g, part, out
        self.base = mail.take(2 + 4 + 8 + 1)
        self.from_sibling, self.sums, self.from_far, self.from_near, self.from_pair = bufs
        self.peers = near(group)

    def steps(self):
        group, mail, part, n = self.g, self.mail, self.part, self.n
        from_sibling, sums, from_far, from_near, from_pair = (
            self.from_sibling.at[n],
            self.sums.at[n],
            self.from_far.at[n],
            self.from_near.at[n],
            self.from_pair.at[n],
        )
        p, t, k = group.p, group.t, group.k
        peers = self.peers
        half = PART // 2
        side = {1: 1 - p, 0: p}
        sib, far, nearby, pair = self.base, self.base + 2, self.base + 6, self.base + 14

        def cell(q, s):
            return pl.multiple_of((side[q] * 4 + (t + s) % RING) * PART, PART)

        def got(number, ref):
            mail.arrived(number, ref, peers["sibling"])

        for q in (1, 0):
            four = pl.ds(pl.multiple_of(side[q] * 4 * PART, 4 * PART), 4 * PART)
            src = part.at[pl.ds(first_row(n, side[q], 0, 1 - k), 4 * PART)]
            mail.send(sib + q, src, from_sibling.at[four], peers["sibling"])
        yield

        def chip_sum(q, s):
            own = first_row(n, side[q], (t + s) % RING, k)
            add_rows(sums, cell(q, s), part, own, from_sibling, cell(q, s), PART)

        for q in (1, 0):
            four = pl.ds(pl.multiple_of(side[q] * 4 * PART, 4 * PART), 4 * PART)
            got(sib + q, from_sibling.at[four])
            chip_sum(q, 2)
            c = cell(q, 2)
            mail.send(far + 2 * q, sums.at[pl.ds(c, half)], from_far.at[2 * q], peers["up"])
            mail.send(
                far + 2 * q + 1, sums.at[pl.ds(c + half, half)], from_far.at[2 * q + 1], peers["down"]
            )
            chip_sum(q, 1)
            low = pl.ds(cell(q, 1) + half, half)
            mail.send(
                nearby + 4 * q, sums.at[low], from_near.at[2 * q, pl.ds(half, half)], peers["up"]
            )
            chip_sum(q, 3)
            top = pl.ds(cell(q, 3), half)
            mail.send(
                nearby + 4 * q + 1, sums.at[top], from_near.at[2 * q + 1, pl.ds(0, half)], peers["down"]
            )
        for q in (1, 0):
            chip_sum(q, 0)
        yield
        for q in (1, 0):
            got(far + 2 * q, from_far.at[2 * q])
            c = cell(q, 1)
            add_rows(sums, c, sums, c, from_far.at[2 * q], 0, half)
            mail.send(
                nearby + 4 * q + 2,
                sums.at[pl.ds(c, half)],
                from_near.at[2 * q, pl.ds(0, half)],
                peers["up"],
            )
            got(far + 2 * q + 1, from_far.at[2 * q + 1])
            c = pl.multiple_of(cell(q, 3) + half, half)
            add_rows(sums, c, sums, c, from_far.at[2 * q + 1], 0, half)
            mail.send(
                nearby + 4 * q + 3,
                sums.at[pl.ds(c, half)],
                from_near.at[2 * q + 1, pl.ds(half, half)],
                peers["down"],
            )
            yield

        def wait_near(q):
            got(nearby + 4 * q, from_near.at[2 * q, pl.ds(half, half)])
            got(nearby + 4 * q + 1, from_near.at[2 * q + 1, pl.ds(0, half)])
            got(nearby + 4 * q + 2, from_near.at[2 * q, pl.ds(0, half)])
            got(nearby + 4 * q + 3, from_near.at[2 * q + 1, pl.ds(half, half)])

        def total(q, i):
            rows = pl.ds(i * 16, 16)
            return (
                sums[pl.ds(cell(q, 0) + i * 16, 16)].astype(f32)
                + from_near[2 * q, rows].astype(f32)
                + from_near[2 * q + 1, rows].astype(f32)
            )

        wait_near(1)

        def pair_part(i, _):
            sums[pl.ds(cell(1, 0) + i * 16, 16)] = total(1, i).astype(b16)
            return 0

        lax.fori_loop(0, PART // 16, pair_part, 0)
        mail.send(pair, sums.at[pl.ds(cell(1, 0), PART)], from_pair, peers["pair"])
        yield
        wait_near(0)
        yield
        got(pair, from_pair)

        def own_part(i, _):
            rows = pl.ds(i * 16, 16)
            self.out[rows] = (total(0, i) + from_pair[rows].astype(f32)).astype(self.out.dtype)
            return 0

        lax.fori_loop(0, PART // 16, own_part, 0)


def scatter_scratch(width):
    return [
        pltpu.VMEM((GROUPS, 8 * PART, width), b16),
        pltpu.VMEM((GROUPS, 8 * PART, width), b16),
        pltpu.VMEM((GROUPS, 4, PART // 2, width), b16),
        pltpu.VMEM((GROUPS, 4, PART, width), b16),
        pltpu.VMEM((GROUPS, PART, width), b16),
    ]


class Swap:
    def __init__(self, place, mail):
        self.place, self.mail, self.number = place, mail, mail.take(1)

    def start(self, src, own_dst, swap_dst):
        self.src, self.dst = src, swap_dst

        @pl.when(self.place.stay)
        def _():
            own_dst[...] = src[...]

        @pl.when(jnp.logical_not(self.place.stay))
        def _():
            self.mail.copy(self.number, src, swap_dst, self.place.swap).start()

    def wait(self):
        @pl.when(jnp.logical_not(self.place.stay))
        def _():
            self.mail.copy(self.number, self.src, self.dst, self.place.swap).wait()


def whole_step(
    pieces, cot, up_one, down_one, up_two, down_two,
    grad_up_one, grad_down_one, grad_up_two, grad_down_two,
    wide, other, inputs, normed_one, slope_one, act_one, part_one,
    cots, up_home, down_home, mixed, middle, mine, normed_two, act_two, slope_two, part_two,
    sum_up_two, sum_down_two, ready_up_two, ready_down_two, back_mine, back, group,
    *scratch,
):
    col_bufs, row_bufs, (send_sem, recv_sem) = scratch[:5], scratch[5:10], scratch[10:]
    place = Place()
    col, row = ColGroup(place), RowGroup(place)
    mail = Mail(send_sem, recv_sem)
    peers_c, peers_r = near(col), near(row)
    greet(
        [peers_c["sibling"], peers_c["pair"], peers_c["up"], peers_c["down"]]
        + [peers_r["pair"], peers_r["up"], peers_r["down"], place.swap]
    )
    k = place.k
    half_rows = ROWS // 2
    my_row = functools.partial(first_row, p=row.p, t=row.t, k=row.k)
    swap_row = functools.partial(first_row, p=row.p, t=row.t, k=1 - row.k)

    def normal_factor(values):
        return lax.rsqrt(jnp.mean(values * values, axis=-1, keepdims=True) + epsilon)

    def rows_of(g, i):
        return pl.ds(pl.multiple_of(g * ROWS + i * CHUNK, CHUNK), CHUNK)

    def accumulate(ref, fresh, value):
        if fresh is True:
            ref[...] = value
        elif fresh is False:
            ref[...] += value

    def chunks(body):
        lax.fori_loop(0, ROWS // CHUNK, lambda i, c: (body(i), c)[1], 0)

    def level_one(g):
        def body(i):
            rows = rows_of(g, i)
            values = inputs[rows].astype(f32)
            normed = (values * normal_factor(values)).astype(b16)
            normed_one[rows] = normed
            act, slope = gelu_and_slope(dot(normed, up_one[...]))
            slope_one[rows] = slope
            act = act.astype(b16)
            act_one[rows] = act
            part_one[rows] = dot(act, down_one[...]).astype(b16)

        chunks(body)

    def level_two(g):
        def body(i):
            rows = rows_of(g, i)
            act, slope = gelu_and_slope(dot(normed_two[rows], up_home[...]))
            act_two[rows] = act.astype(b16)
            slope = (slope * dot_cols(cots[rows], down_home[...])).astype(b16)
            slope_two[rows] = slope
            part_two[rows] = dot_cols(slope, up_home[...]).astype(b16)

        chunks(body)

    def level_two_grads(g):
        def body(i):
            rows = rows_of(g, i)
            sum_down_two[...] += dot_rows(act_two[rows], cots[rows])
            sum_up_two[...] += dot_rows(slope_two[rows], normed_two[rows])

        chunks(body)

    def level_one_back(g):
        def body(i):
            rows = rows_of(g, i)
            upstream = group[rows]
            grad_down_one[...] += dot_rows(act_one[rows], upstream)
            slope = (slope_one[rows] * dot_cols(upstream, down_one[...])).astype(b16)
            grad_up_one[...] += dot_rows(slope, normed_one[rows])

        chunks(body)

    swaps = {name: Swap(place, mail) for name in ("cot", "up", "down", "grad_up", "grad_down")}

    def chain(g):
        number = mail.take(1)
        own = pieces[pl.ds(g * ROWS, ROWS)]
        wide[pl.ds(g * ROWS, ROWS)] = jnp.concatenate([own, own], axis=1)
        there = pl.ds(pl.multiple_of(g * ROWS + (1 - k) * half_rows, half_rows), half_rows)
        here = pl.ds(pl.multiple_of(g * ROWS + k * half_rows, half_rows), half_rows)
        landed = other.at[pl.ds(g * half_rows, half_rows)]
        mail.send(number, wide.at[there], landed, peers_c["sibling"])
        yield
        mail.arrived(number, landed, peers_c["sibling"])
        lane = lax.broadcasted_iota(jnp.int32, (half_rows, 128), 1) // 64

        def lanes(p, t):
            return pl.ds(pl.multiple_of((p * 4 + t) * 128, 128), 128)

        inputs[here, lanes(col.p, col.t)] = jnp.where(lane == k, wide[here], landed[...])

        def region(p, t, k):
            at = pl.multiple_of(g * ROWS + k * half_rows, half_rows)
            return inputs.at[pl.ds(at, half_rows), lanes(p, t)]

        def half(p, t, k, h):
            quarter = half_rows // 2
            at = pl.multiple_of(g * ROWS + k * half_rows + h * quarter, quarter)
            return inputs.at[pl.ds(at, quarter), lanes(p, t)]

        yield from Gather(col, mail, region, half).steps()
        level_one(g)
        yield from Scatter(col, mail, g, part_one, col_bufs, mixed).steps()
        own_input = inputs[pl.ds(first_row(g, col.p, col.t, col.k), PART)]
        values = own_input.astype(f32) + mixed[...]
        middle[g] = values
        mine[g] = (values * normal_factor(values)).astype(b16)
        swap = Swap(place, mail)
        swap.start(
            mine.at[g],
            normed_two.at[pl.ds(my_row(g), PART)],
            normed_two.at[pl.ds(swap_row(g), PART)],
        )
        yield
        swap.wait()
        yield from Gather(row, mail, *token_regions(normed_two, g)).steps()
        if g == 0:
            swaps["up"].wait()
            swaps["down"].wait()
        level_two(g)
        scatter = Scatter(row, mail, g, part_two, row_bufs, back_mine.at[g]).steps()
        next(scatter)
        yield
        next(scatter)
        level_two_grads(g)
        yield
        if g == GROUPS - 1:
            ready_up_two[...] = sum_up_two[...].astype(b16)
            ready_down_two[...] = sum_down_two[...].astype(b16)
            swaps["grad_up"].start(ready_up_two, grad_up_two, grad_up_two)
            swaps["grad_down"].start(ready_down_two, grad_down_two, grad_down_two)
        yield from scatter
        swap = Swap(place, mail)
        swap.start(back_mine.at[g], back.at[g], back.at[g])
        yield
        swap.wait()
        upstream = back[g].astype(f32)
        values = middle[g]
        factor = normal_factor(values)
        through = factor * upstream - values * (factor * factor * factor) * jnp.mean(
            upstream * values, axis=-1, keepdims=True
        )
        own_cot = cot[pl.ds(g * PART, PART)].astype(f32)
        group[pl.ds(first_row(g, col.p, col.t, col.k), PART)] = (own_cot + through).astype(b16)
        yield from Gather(col, mail, *token_regions(group, g)).steps()
        level_one_back(g)

    def background():
        for ref in (grad_up_one, grad_down_one, sum_up_two, sum_down_two):
            ref[...] = jnp.zeros_like(ref)
        cot_swaps = [Swap(place, mail) for _ in range(GROUPS)]
        for g, swap in enumerate(cot_swaps):
            swap.start(
                cot.at[pl.ds(g * PART, PART)],
                cots.at[pl.ds(my_row(g), PART)],
                cots.at[pl.ds(swap_row(g), PART)],
            )
        yield
        swaps["up"].start(up_two, up_home, up_home)
        swaps["down"].start(down_two, down_home, down_home)
        for g, swap in enumerate(cot_swaps):
            swap.wait()
        gathers = [Gather(row, mail, *token_regions(cots, g)).steps() for g in range(GROUPS)]
        while gathers:
            gathers = [gather for gather in gathers if next(gather, "done") != "done"]
            yield

    tasks = [(0, chain(0)), (1, background())] + [(LAG * g, chain(g)) for g in range(1, GROUPS)]
    tick = 0
    while tasks:
        left = []
        for begin, task in tasks:
            if tick < begin or next(task, "done") != "done":
                left.append((begin, task))
        tasks = left
        tick += 1
    swaps["grad_up"].wait()
    swaps["grad_down"].wait()
    mail.finish()


def on_device(
    token_ids,
    embedding,
    up_one,
    down_one,
    up_two,
    down_two,
    moment_up_one,
    moment_down_one,
    moment_up_two,
    moment_down_two,
    cotangent,
):
    sharers = PATHS
    width, hidden = up_one.shape[1:]
    ids = token_ids[0].reshape(2, 4, 2, GROUPS, PART).transpose(3, 2, 0, 1, 4).reshape(-1)
    count = ids.shape[0]
    pieces = embedding.at[ids].get(mode="promise_in_bounds")
    vmem = pl.BlockSpec(memory_space=pltpu.VMEM)
    args = [pieces, cotangent[0, 0], up_one[0], down_one[0], up_two[0], down_two[0]]
    out_shape = [jax.ShapeDtypeStruct((hidden, width), f32)] * 2
    out_shape += [jax.ShapeDtypeStruct((hidden, width), b16)] * 2
    tokens_b16 = pltpu.VMEM((count, width), b16)
    part_b16 = pltpu.VMEM((GROUPS, PART, width), b16)
    hidden_b16 = pltpu.VMEM((count, hidden), b16)
    grad_f32 = pltpu.VMEM((hidden, width), f32)
    grad_b16 = pltpu.VMEM((hidden, width), b16)
    scratch = [
        pltpu.VMEM((count, 128), b16),
        pltpu.VMEM((count // 2, 128), b16),
        tokens_b16,
        tokens_b16,
        pltpu.VMEM((count, hidden), f32),
        hidden_b16,
        tokens_b16,
        tokens_b16,
        pltpu.VMEM((width, hidden), b16),
        pltpu.VMEM((hidden, width), b16),
        pltpu.VMEM((PART, width), f32),
        pltpu.VMEM((GROUPS, PART, width), f32),
        part_b16,
        tokens_b16,
        hidden_b16,
        hidden_b16,
        tokens_b16,
        grad_f32,
        grad_f32,
        grad_b16,
        grad_b16,
        part_b16,
        part_b16,
        tokens_b16,
    ]
    scratch += scatter_scratch(width) + scatter_scratch(width)
    messages = GROUPS * (1 + 17 + 15 + 1 + 17 + 15 + 1 + 17 + 1 + 17) + 5
    scratch += [pltpu.SemaphoreType.DMA((messages,)), pltpu.SemaphoreType.DMA((messages,))]
    grad_up_one, grad_down_one, grad_up_two, grad_down_two = pl.pallas_call(
        whole_step,
        name="whole_step",
        out_shape=out_shape,
        in_specs=[vmem] * len(args),
        out_specs=[vmem] * len(out_shape),
        scratch_shapes=scratch,
        compiler_params=pltpu.CompilerParams(
            collective_id=0, has_side_effects=True, vmem_limit_bytes=60 * 2**20
        ),
    )(*args)
    new_up_one, new_moment_up_one = outer_update(
        up_one[0], moment_up_one[0], grad_up_one.T, sharers
    )
    new_down_one, new_moment_down_one = outer_update(
        down_one[0], moment_down_one[0], grad_down_one, sharers
    )
    new_up_two, new_moment_up_two = outer_update(
        up_two[0], moment_up_two[0], grad_up_two.T.astype(f32), sharers
    )
    new_down_two, new_moment_down_two = outer_update(
        down_two[0], moment_down_two[0], grad_down_two.astype(f32), sharers
    )
    return (
        new_up_one,
        new_down_one,
        new_up_two,
        new_down_two,
        new_moment_up_one,
        new_moment_down_one,
        new_moment_up_two,
        new_moment_down_two,
    )


def solution(mesh):
    in_specs = (
        P("row", None, None),
        P(None, "col"),
        P("row", None, "col"),
        P("row", "col", None),
        P("col", None, "row"),
        P("col", "row", None),
        P("row", None, "col"),
        P("row", "col", None),
        P("col", None, "row"),
        P("col", "row", None),
        P("row", "col", None, None),
    )
    out_specs = (
        P("row", None, "col"),
        P("row", "col", None),
        P("col", None, "row"),
        P("col", "row", None),
        P("row", None, "col"),
        P("row", "col", None),
        P("col", None, "row"),
        P("col", "row", None),
    )
    return jax.shard_map(
        on_device, mesh=mesh, in_specs=in_specs, out_specs=out_specs, check_vma=False
    )
```

```python
import functools

import jax
import jax.numpy as jnp
from jax import lax
from jax.experimental import pallas as pl
from jax.experimental.pallas import tpu as pltpu
from jax.sharding import PartitionSpec as P

epsilon = 1e-06
momentum_decay = 0.9
outer_rate = 0.7
inner_rate = 0.01
MESH = pl.DeviceIdType.MESH
RING = 4
PATHS = 16
TOKENS = 128
GROUPS = 2
PART = TOKENS // GROUPS
ROWS = PATHS * PART
ORDER = (
    0, 1, 2, 2, 0, 1, 2, 2, 0, 1, 0, 2, 2, 2, 1, 0, 0, 2, 1, 1, 2, 2, 0, 0, 1, 2, 2, 0, 0, 1,
    0, 2, 0, 1, 1, 2, 0, 0, 1, 1, 0, 1, 1, 0, 0, 1, 0, 1, 0, 0, 1, 1, 0, 0, 1, 1, 0, 0, 1, 0,
    1, 0, 0, 1, 1, 0, 1, 0, 1, 1, 0, 1, 1, 0, 0, 1, 0, 0, 1, 0, 1, 0, 1, 1, 1, 1,
)
CHUNK = 256
COLLECTIVE = 0
LATE = 2
f32, b16 = jnp.float32, jnp.bfloat16


def update_kernel(sharers, *refs):
    grads, weights, moments, new_weights, new_moments = (refs[4 * i : 4 * i + 4] for i in range(5))
    for i in range(4):
        gradient = grads[i][...].astype(f32)
        if i % 2 == 0:
            gradient = gradient.T
        average = gradient * (1.0 / sharers)
        new_moment = momentum_decay * moments[i][...].astype(f32) + average
        new_moments[i][0] = new_moment.astype(b16)
        new_weights[i][0] = (
            weights[i][...].astype(f32)
            - outer_rate * inner_rate * (average + momentum_decay * new_moment)
        ).astype(b16)


def update(grads, weights, moments, sharers):
    hidden, width = weights[1].shape
    block = hidden // 2
    up = pl.BlockSpec((width, block), lambda i: (0, i))
    down = pl.BlockSpec((block, width), lambda i: (i, 0))
    new_up = pl.BlockSpec((1, width, block), lambda i: (0, 0, i))
    new_down = pl.BlockSpec((1, block, width), lambda i: (0, i, 0))
    return pl.pallas_call(
        functools.partial(update_kernel, sharers),
        name="update",
        grid=(2,),
        out_shape=[jax.ShapeDtypeStruct((1,) + w.shape, b16) for w in weights] * 2,
        in_specs=[down] * 4 + [up, down, up, down] * 2,
        out_specs=[new_up, new_down, new_up, new_down] * 2,
        compiler_params=pltpu.CompilerParams(vmem_limit_bytes=60 * 2**20),
    )(*grads, *weights, *moments)


def swap_pairs():
    pairs = []
    for zl in range(4):
        for x in range(4):
            for col in range(16):
                if zl // 2 != col % 2:
                    source = (zl * 4 + x) * 16 + col
                    pairs.append((source, ((zl + 2) % 4 * 4 + x) * 16 + (col ^ 1)))
    return pairs


def gelu_and_slope(v):
    scale, cubic = 0.7978845608028654, 0.044715
    square = v * v
    t = jnp.tanh(scale * v * (1.0 + cubic * square))
    half = 0.5 * (1.0 + t)
    slope = half + 0.5 * v * (1.0 - t * t) * (scale * (1.0 + 3.0 * cubic * square))
    return v * half, slope


def dot(a, b):
    return jnp.dot(a, b, preferred_element_type=f32)


def dot_rows(a, b):
    return lax.dot_general(a, b, (((0,), (0,)), ((), ())), preferred_element_type=f32)


def dot_cols(a, b):
    return lax.dot_general(a, b, (((1,), (1,)), ((), ())), preferred_element_type=f32)


class Place:
    def __init__(self):
        row, col = lax.axis_index("row"), lax.axis_index("col")
        self.zl, self.x = row // 4, row % 4
        self.zh, self.y, self.k = col // 8, (col // 2) % 4, col % 2
        self.stay = (self.zl // 2) == self.k
        other_zl = (self.zl + 2) % 4
        self.swap = (other_zl * 4 + self.x, self.zh * 8 + self.y * 2 + (1 - self.k))


class ColGroup:
    def __init__(self, place):
        self.place = place
        self.p, self.t, self.k = place.zh, place.y, place.k

    def device(self, p, t, k):
        return (self.place.zl * 4 + self.place.x, p * 8 + t * 2 + k)


class RowGroup:
    def __init__(self, place):
        self.place = place
        self.p, self.t, self.k = place.zl % 2, place.x, place.k
        self.half = place.zl // 2

    def device(self, p, t, k):
        return ((self.half * 2 + p) * 4 + t, self.place.zh * 8 + self.place.y * 2 + k)


def slot(p, t, k):
    return k * 8 + p * 4 + t


def first_row(g, p, t, k):
    return pl.multiple_of((g * PATHS + slot(p, t, k)) * PART, PART)


def near(group):
    p, t, k = group.p, group.t, group.k
    up, down = (t + 1) % RING, (t + RING - 1) % RING
    return {
        "pair": group.device(1 - p, t, k),
        "sibling": group.device(p, t, 1 - k),
        "up": group.device(p, up, k),
        "down": group.device(p, down, k),
    }


def greet(devices):
    barrier = pltpu.get_barrier_semaphore()
    for device in devices:
        pl.semaphore_signal(barrier, inc=1, device_id=device, device_id_type=MESH)
    pl.semaphore_wait(barrier, len(devices))


class Mail:
    def __init__(self, send_sem, recv_sem):
        self.send_sem, self.recv_sem = send_sem, recv_sem
        self.sent = []
        self.used = 0
        self.notes = []

    def note(self, mark):
        self.notes.append(mark)

    def take(self, count):
        self.used += count
        return self.used - count

    def copy(self, number, src, dst, device):
        return pltpu.make_async_remote_copy(
            src_ref=src,
            dst_ref=dst,
            send_sem=self.send_sem.at[number],
            recv_sem=self.recv_sem.at[number],
            device_id=device,
            device_id_type=MESH,
        )

    def send(self, number, src, dst, device):
        copy = self.copy(number, src, dst, device)
        copy.start()
        self.sent.append(copy)

    def arrived(self, number, ref, device):
        self.copy(number, ref, ref, device).wait_recv()

    def finish(self):
        for copy in self.sent:
            copy.wait_send()
        self.sent = []


class Gather:
    def __init__(self, group, mail, region, half):
        self.g, self.mail, self.region, self.half = group, mail, region, half
        self.base = mail.take(17)
        self.peers = near(group)

    def send(self, m, ref, to):
        self.mail.send(self.base + m, ref, ref, self.peers[to])

    def numbers(self, *messages):
        return [self.base + m for m in messages]

    def got(self, m, ref):
        self.mail.arrived(self.base + m, ref, self.peers["sibling"])

    def steps(self):
        g = self.g
        p, t, k = g.p, g.t, g.k
        before, after, far = (t + RING - 1) % RING, (t + 1) % RING, (t + 2) % RING
        own = self.region(p, t, k)
        self.send(0, own, "pair")
        self.send(2, own, "up")
        self.send(3, own, "down")
        self.send(1, own, "sibling")
        yield self.numbers(2, 3)
        for q, first, fwd in ((p, 2, 7), (1 - p, 4, 11)):
            if first == 4:
                ref = self.region(q, t, k)
                self.got(0, ref)
                self.send(4, ref, "up")
                self.send(5, ref, "down")
                self.send(6, ref, "sibling")
                yield self.numbers(4, 5)
            ref = self.region(q, before, k)
            self.got(first, ref)
            self.send(fwd, self.half(q, before, k, 0), "up")
            self.send(fwd + 1, ref, "sibling")
            ref = self.region(q, after, k)
            self.got(first + 1, ref)
            self.send(fwd + 2, self.half(q, after, k, 1), "down")
            self.send(fwd + 3, ref, "sibling")
            yield self.numbers(0) if first == 2 else self.numbers(7, 9)
        for q, fwd, last in ((p, 7, 15), (1 - p, 11, 16)):
            self.got(fwd, self.half(q, far, k, 0))
            self.got(fwd + 2, self.half(q, far, k, 1))
            self.send(last, self.region(q, far, k), "sibling")
            yield self.numbers(11, 13) if last == 15 else self.numbers(1, 6, 8, 10, 12, 14, 15, 16)
        for m, q, s in (
            (1, p, t),
            (6, 1 - p, t),
            (8, p, before),
            (10, p, after),
            (12, 1 - p, before),
            (14, 1 - p, after),
            (15, p, far),
            (16, 1 - p, far),
        ):
            self.got(m, self.region(q, s, 1 - k))


def token_regions(buf, g):
    def region(p, t, k):
        return buf.at[pl.ds(first_row(g, p, t, k), PART)]

    def half(p, t, k, h):
        return buf.at[pl.ds(first_row(g, p, t, k) + h * (PART // 2), PART // 2)]

    return region, half


def add_rows(dst, at, left, left_at, right, right_at, count):
    step = 16

    def body(i, _):
        off = i * step
        dst[pl.ds(at + off, step)] = (
            left[pl.ds(left_at + off, step)].astype(f32)
            + right[pl.ds(right_at + off, step)].astype(f32)
        ).astype(b16)
        return 0

    lax.fori_loop(0, count // step, body, 0, unroll=2)


class Scatter:
    def __init__(self, group, mail, g, part, bufs, out):
        self.g, self.mail, self.n, self.part, self.out = group, mail, g, part, out
        self.base = mail.take(2 + 4 + 8 + 1)
        self.from_sibling, self.sums, self.from_far, self.from_near, self.from_pair = bufs
        self.peers = near(group)

    def steps(self):
        group, mail, part, n = self.g, self.mail, self.part, self.n
        from_sibling, sums, from_far, from_near, from_pair = (
            self.from_sibling.at[n],
            self.sums.at[n],
            self.from_far.at[n],
            self.from_near.at[n],
            self.from_pair.at[n],
        )
        p, t, k = group.p, group.t, group.k
        peers = self.peers
        half = PART // 2
        side = {1: 1 - p, 0: p}
        sib, far, nearby, pair = self.base, self.base + 2, self.base + 6, self.base + 14

        def cell(q, s):
            return pl.multiple_of((side[q] * 4 + (t + s) % RING) * PART, PART)

        def got(number, ref):
            mail.arrived(number, ref, peers["sibling"])

        for q in (1, 0):
            four = pl.ds(pl.multiple_of(side[q] * 4 * PART, 4 * PART), 4 * PART)
            src = part.at[pl.ds(first_row(n, side[q], 0, 1 - k), 4 * PART)]
            mail.send(sib + q, src, from_sibling.at[four], peers["sibling"])
        yield [sib + 1]

        def chip_sum(q, s):
            own = first_row(n, side[q], (t + s) % RING, k)
            add_rows(sums, cell(q, s), part, own, from_sibling, cell(q, s), PART)

        for q in (1, 0):
            if q == 0:
                yield [sib]
            four = pl.ds(pl.multiple_of(side[q] * 4 * PART, 4 * PART), 4 * PART)
            got(sib + q, from_sibling.at[four])
            chip_sum(q, 2)
            c = cell(q, 2)
            mail.send(far + 2 * q, sums.at[pl.ds(c, half)], from_far.at[2 * q], peers["up"])
            mail.send(
                far + 2 * q + 1, sums.at[pl.ds(c + half, half)], from_far.at[2 * q + 1], peers["down"]
            )
            chip_sum(q, 1)
            low = pl.ds(cell(q, 1) + half, half)
            mail.send(
                nearby + 4 * q, sums.at[low], from_near.at[2 * q, pl.ds(half, half)], peers["up"]
            )
            chip_sum(q, 3)
            top = pl.ds(cell(q, 3), half)
            mail.send(
                nearby + 4 * q + 1, sums.at[top], from_near.at[2 * q + 1, pl.ds(0, half)], peers["down"]
            )
        for q in (1, 0):
            chip_sum(q, 0)
        for q in (1, 0):
            yield [far + 2 * q, far + 2 * q + 1]
            got(far + 2 * q, from_far.at[2 * q])
            c = cell(q, 1)
            add_rows(sums, c, sums, c, from_far.at[2 * q], 0, half)
            mail.send(
                nearby + 4 * q + 2,
                sums.at[pl.ds(c, half)],
                from_near.at[2 * q, pl.ds(0, half)],
                peers["up"],
            )
            got(far + 2 * q + 1, from_far.at[2 * q + 1])
            c = pl.multiple_of(cell(q, 3) + half, half)
            add_rows(sums, c, sums, c, from_far.at[2 * q + 1], 0, half)
            mail.send(
                nearby + 4 * q + 3,
                sums.at[pl.ds(c, half)],
                from_near.at[2 * q + 1, pl.ds(half, half)],
                peers["down"],
            )

        def wait_near(q):
            got(nearby + 4 * q, from_near.at[2 * q, pl.ds(half, half)])
            got(nearby + 4 * q + 1, from_near.at[2 * q + 1, pl.ds(0, half)])
            got(nearby + 4 * q + 2, from_near.at[2 * q, pl.ds(0, half)])
            got(nearby + 4 * q + 3, from_near.at[2 * q + 1, pl.ds(half, half)])

        def total(q, i):
            rows = pl.ds(i * 16, 16)
            return (
                sums[pl.ds(cell(q, 0) + i * 16, 16)].astype(f32)
                + from_near[2 * q, rows].astype(f32)
                + from_near[2 * q + 1, rows].astype(f32)
            )

        yield [nearby + 4 + i for i in range(4)]
        wait_near(1)

        def pair_part(i, _):
            sums[pl.ds(cell(1, 0) + i * 16, 16)] = total(1, i).astype(b16)
            return 0

        lax.fori_loop(0, PART // 16, pair_part, 0)
        mail.send(pair, sums.at[pl.ds(cell(1, 0), PART)], from_pair, peers["pair"])
        yield [nearby + i for i in range(4)]
        wait_near(0)
        yield [pair]
        got(pair, from_pair)

        def own_part(i, _):
            rows = pl.ds(i * 16, 16)
            self.out[rows] = (total(0, i) + from_pair[rows].astype(f32)).astype(self.out.dtype)
            return 0

        lax.fori_loop(0, PART // 16, own_part, 0)


def scatter_scratch(width):
    return [
        pltpu.VMEM((GROUPS, 8 * PART, width), b16),
        pltpu.VMEM((GROUPS, 8 * PART, width), b16),
        pltpu.VMEM((GROUPS, 4, PART // 2, width), b16),
        pltpu.VMEM((GROUPS, 4, PART, width), b16),
        pltpu.VMEM((GROUPS, PART, width), b16),
    ]


class Swap:
    def __init__(self, place, mail):
        self.place, self.mail, self.number = place, mail, mail.take(1)

    def start(self, src, own_dst, swap_dst):
        self.src, self.dst = src, swap_dst

        @pl.when(self.place.stay)
        def _():
            own_dst[...] = src[...]

        @pl.when(jnp.logical_not(self.place.stay))
        def _():
            self.mail.copy(self.number, src, swap_dst, self.place.swap).start()

    def wait(self):
        @pl.when(jnp.logical_not(self.place.stay))
        def _():
            self.mail.copy(self.number, self.src, self.dst, self.place.swap).wait()


def whole_step(
    pieces, cot, up_one, down_one, up_two, down_two, cot_other, up_other, down_other,
    grad_up_one, grad_down_one, grad_up_two, grad_down_two,
    wide, other, inputs, normed_one, slope_one, act_one, part_one,
    cots, up_home, down_home, mixed, middle, mine, normed_two, act_two, slope_two, part_two,
    sum_up_two, sum_down_two, ready_up_two, ready_down_two, back_mine, back, group,
    *scratch,
):
    col_bufs, row_bufs, (send_sem, recv_sem) = scratch[:5], scratch[5:10], scratch[10:]
    place = Place()
    col, row = ColGroup(place), RowGroup(place)
    mail = Mail(send_sem, recv_sem)
    peers_c, peers_r = near(col), near(row)
    greet(
        [peers_c["sibling"], peers_c["pair"], peers_c["up"], peers_c["down"]]
        + [peers_r["pair"], peers_r["up"], peers_r["down"], place.swap]
    )
    k = place.k
    half_rows = ROWS // 2
    my_row = functools.partial(first_row, p=row.p, t=row.t, k=row.k)
    swap_row = functools.partial(first_row, p=row.p, t=row.t, k=1 - row.k)

    def normal_factor(values):
        return lax.rsqrt(jnp.mean(values * values, axis=-1, keepdims=True) + epsilon)

    def rows_of(g, i):
        return pl.ds(pl.multiple_of(g * ROWS + i * CHUNK, CHUNK), CHUNK)

    def accumulate(ref, fresh, value):
        if fresh is True:
            ref[...] = value
        elif fresh is False:
            ref[...] += value

    def chunks(body):
        lax.fori_loop(0, ROWS // CHUNK, lambda i, c: (body(i), c)[1], 0)

    def level_one(g):
        def body(i):
            rows = rows_of(g, i)
            values = inputs[rows].astype(f32)
            normed = (values * normal_factor(values)).astype(b16)
            normed_one[rows] = normed
            act, slope = gelu_and_slope(dot(normed, up_one[...]))
            slope_one[rows] = slope
            act = act.astype(b16)
            act_one[rows] = act
            part_one[rows] = dot(act, down_one[...]).astype(b16)

        chunks(body)

    def level_two(g):
        def body(i):
            rows = rows_of(g, i)
            act, slope = gelu_and_slope(dot(normed_two[rows], up_home[...]))
            act_two[rows] = act.astype(b16)
            slope = (slope * dot_cols(cots[rows], down_home[...])).astype(b16)
            slope_two[rows] = slope
            part_two[rows] = dot_cols(slope, up_home[...]).astype(b16)

        chunks(body)

    def level_two_grads(g):
        def body(i):
            rows = rows_of(g, i)
            sum_down_two[...] += dot_rows(act_two[rows], cots[rows])
            sum_up_two[...] += dot_rows(slope_two[rows], normed_two[rows])

        chunks(body)

    def level_one_back(g):
        def body(i):
            rows = rows_of(g, i)
            upstream = group[rows]
            grad_down_one[...] += dot_rows(act_one[rows], upstream)
            slope = (slope_one[rows] * dot_cols(upstream, down_one[...])).astype(b16)
            grad_up_one[...] += dot_rows(slope, normed_one[rows])

        chunks(body)

    swaps = {name: Swap(place, mail) for name in ("grad_up", "grad_down")}

    def chain(g):
        number = mail.take(1)
        for path in range(PATHS):
            own = pieces[pl.ds(path * TOKENS + g * PART, PART)]
            to = g * ROWS + slot(path // 8, path // 2 % RING, path % 2) * PART
            wide[pl.ds(to, PART)] = jnp.concatenate([own, own], axis=1)
        there = pl.ds(pl.multiple_of(g * ROWS + (1 - k) * half_rows, half_rows), half_rows)
        here = pl.ds(pl.multiple_of(g * ROWS + k * half_rows, half_rows), half_rows)
        landed = other.at[pl.ds(g * half_rows, half_rows)]
        mail.send(number, wide.at[there], landed, peers_c["sibling"])
        yield [number]
        mail.arrived(number, landed, peers_c["sibling"])
        lane = lax.broadcasted_iota(jnp.int32, (half_rows, 128), 1) // 64

        def lanes(p, t):
            return pl.ds(pl.multiple_of((p * 4 + t) * 128, 128), 128)

        inputs[here, lanes(col.p, col.t)] = jnp.where(lane == k, wide[here], landed[...])

        def region(p, t, k):
            at = pl.multiple_of(g * ROWS + k * half_rows, half_rows)
            return inputs.at[pl.ds(at, half_rows), lanes(p, t)]

        def half(p, t, k, h):
            quarter = half_rows // 2
            at = pl.multiple_of(g * ROWS + k * half_rows + h * quarter, quarter)
            return inputs.at[pl.ds(at, quarter), lanes(p, t)]

        yield from Gather(col, mail, region, half).steps()
        level_one(g)
        yield from Scatter(col, mail, g, part_one, col_bufs, mixed).steps()
        own_input = inputs[pl.ds(first_row(g, col.p, col.t, col.k), PART)]
        values = own_input.astype(f32) + mixed[...]
        middle[g] = values
        mine[g] = (values * normal_factor(values)).astype(b16)
        swap = Swap(place, mail)
        swap.start(
            mine.at[g],
            normed_two.at[pl.ds(my_row(g), PART)],
            normed_two.at[pl.ds(swap_row(g), PART)],
        )
        yield [swap.number]
        swap.wait()
        yield from Gather(row, mail, *token_regions(normed_two, g)).steps()
        if -1 - g not in mail.notes:
            yield [-1 - g]
        assert -1 - g in mail.notes
        level_two(g)
        scatter = Scatter(row, mail, g, part_two, row_bufs, back_mine.at[g]).steps()
        yield next(scatter)
        yield next(scatter)
        awaited = next(scatter)
        level_two_grads(g)
        yield awaited
        yield from scatter
        swap = Swap(place, mail)
        swap.start(back_mine.at[g], back.at[g], back.at[g])
        yield [swap.number]
        swap.wait()
        upstream = back[g].astype(f32)
        values = middle[g]
        factor = normal_factor(values)
        through = factor * upstream - values * (factor * factor * factor) * jnp.mean(
            upstream * values, axis=-1, keepdims=True
        )
        own_cot = cot[pl.ds(g * PART, PART)].astype(f32)
        group[pl.ds(first_row(g, col.p, col.t, col.k), PART)] = (own_cot + through).astype(b16)
        for step, awaited in enumerate(Gather(col, mail, *token_regions(group, g)).steps()):
            if step == LATE and g == GROUPS - 1:
                ready_up_two[...] = sum_up_two[...].astype(b16)
                ready_down_two[...] = sum_down_two[...].astype(b16)
                swaps["grad_up"].start(ready_up_two, grad_up_two, grad_up_two)
                swaps["grad_down"].start(ready_down_two, grad_down_two, grad_down_two)
            yield awaited
        level_one_back(g)

    def keep_or_take(dst, own, other):
        @pl.when(place.stay)
        def _():
            dst[...] = own[...]

        @pl.when(jnp.logical_not(place.stay))
        def _():
            dst[...] = other[...]

    def background():
        for ref in (grad_up_one, grad_down_one, sum_up_two, sum_down_two):
            ref[...] = jnp.zeros_like(ref)
        for g in range(GROUPS):
            keep_or_take(
                cots.at[pl.ds(my_row(g), PART)],
                cot.at[pl.ds(g * PART, PART)],
                cot_other.at[pl.ds(g * PART, PART)],
            )
        keep_or_take(up_home, up_two, up_other)
        keep_or_take(down_home, down_two, down_other)
        yield []
        for g in range(GROUPS):
            yield from Gather(row, mail, *token_regions(cots, g)).steps()
            mail.note(-1 - g)

    tasks = [chain(g) for g in range(GROUPS)] + [background()]
    for task in ORDER:
        next(tasks[int(task)], None)
    swaps["grad_up"].wait()
    swaps["grad_down"].wait()
    mail.finish()


def gradients(*args):
    vmem = pl.BlockSpec(memory_space=pltpu.VMEM)
    width, hidden = args[2].shape
    count = args[0].shape[0]
    out_shape = [jax.ShapeDtypeStruct((hidden, width), f32)] * 2
    out_shape += [jax.ShapeDtypeStruct((hidden, width), b16)] * 2
    tokens_b16 = pltpu.VMEM((count, width), b16)
    part_b16 = pltpu.VMEM((GROUPS, PART, width), b16)
    hidden_b16 = pltpu.VMEM((count, hidden), b16)
    grad_f32 = pltpu.VMEM((hidden, width), f32)
    grad_b16 = pltpu.VMEM((hidden, width), b16)
    scratch = [
        pltpu.VMEM((count, 128), b16),
        pltpu.VMEM((count // 2, 128), b16),
        tokens_b16,
        tokens_b16,
        pltpu.VMEM((count, hidden), f32),
        hidden_b16,
        tokens_b16,
        tokens_b16,
        pltpu.VMEM((width, hidden), b16),
        pltpu.VMEM((hidden, width), b16),
        pltpu.VMEM((PART, width), f32),
        pltpu.VMEM((GROUPS, PART, width), f32),
        part_b16,
        tokens_b16,
        hidden_b16,
        hidden_b16,
        tokens_b16,
        grad_f32,
        grad_f32,
        grad_b16,
        grad_b16,
        part_b16,
        part_b16,
        tokens_b16,
    ]
    scratch += scatter_scratch(width) + scatter_scratch(width)
    messages = GROUPS * (1 + 17 + 15 + 1 + 17 + 15 + 1 + 17 + 17) + 2
    scratch += [pltpu.SemaphoreType.DMA((messages,)), pltpu.SemaphoreType.DMA((messages,))]
    return pl.pallas_call(
        whole_step,
        name="whole_step",
        out_shape=out_shape,
        in_specs=[vmem] * len(args),
        out_specs=[vmem] * len(out_shape),
        scratch_shapes=scratch,
        compiler_params=pltpu.CompilerParams(
            collective_id=COLLECTIVE, has_side_effects=True, vmem_limit_bytes=60 * 2**20
        ),
    )(*args)


def on_device(
    token_ids,
    embedding,
    up_one,
    down_one,
    up_two,
    down_two,
    moment_up_one,
    moment_down_one,
    moment_up_two,
    moment_down_two,
    cotangent,
):
    sharers = PATHS
    ids = token_ids[0].reshape(-1)
    pieces = embedding.at[ids].get(mode="promise_in_bounds")
    own = (cotangent[0, 0], up_two[0], down_two[0])
    pairs = swap_pairs()
    other = [lax.ppermute(part, ("row", "col"), pairs) for part in own]
    grads = gradients(pieces, own[0], up_one[0], down_one[0], own[1], own[2], *other)
    return update(
        grads,
        (up_one[0], down_one[0], up_two[0], down_two[0]),
        (moment_up_one[0], moment_down_one[0], moment_up_two[0], moment_down_two[0]),
        sharers,
    )


def solution(mesh):
    in_specs = (
        P("row", None, None),
        P(None, "col"),
        P("row", None, "col"),
        P("row", "col", None),
        P("col", None, "row"),
        P("col", "row", None),
        P("row", None, "col"),
        P("row", "col", None),
        P("col", None, "row"),
        P("col", "row", None),
        P("row", "col", None, None),
    )
    out_specs = (
        P("row", None, "col"),
        P("row", "col", None),
        P("col", None, "row"),
        P("col", "row", None),
        P("row", None, "col"),
        P("row", "col", None),
        P("col", None, "row"),
        P("col", "row", None),
    )
    return jax.shard_map(
        on_device, mesh=mesh, in_specs=in_specs, out_specs=out_specs, check_vma=False
    )
```

```python
import functools

import jax
import jax.numpy as jnp
from jax import lax
from jax.experimental import pallas as pl
from jax.experimental.pallas import tpu as pltpu
from jax.sharding import PartitionSpec as P

epsilon = 1e-06
momentum_decay = 0.9
outer_rate = 0.7
inner_rate = 0.01
MESH = pl.DeviceIdType.MESH
RING = 4
PATHS = 16
TOKENS = 128
GROUPS = 2
PART = TOKENS // GROUPS
ROWS = PATHS * PART
ORDER = (
    0, 1, 2, 0, 1, 2, 0, 1, 2, 0, 1, 0, 0, 1, 1, 2, 0, 0, 1, 2, 2, 0, 0, 1, 0, 2, 0, 1, 1, 2,
    0, 0, 1, 2, 1, 2, 1, 1, 2, 2, 0, 2, 2, 1, 0, 1, 0, 1, 0, 0, 0, 1, 0, 0, 0, 1, 1, 0, 0, 1,
    0, 1, 0, 0, 1, 1, 0, 1, 1, 0, 1, 1, 0, 0, 1, 0, 1, 0, 0, 1, 1, 0, 0, 1, 1, 1, 1,
)
CHUNK = 256
COLLECTIVE = 0
LATE = 1
EARLY = 1
f32, b16 = jnp.float32, jnp.bfloat16


def update_kernel(sharers, *refs):
    grads, weights, moments, new_weights, new_moments = (refs[4 * i : 4 * i + 4] for i in range(5))
    for i in range(4):
        gradient = grads[i][...].astype(f32)
        if i % 2 == 0:
            gradient = gradient.T
        average = gradient * (1.0 / sharers)
        new_moment = momentum_decay * moments[i][...].astype(f32) + average
        new_moments[i][0] = new_moment.astype(b16)
        new_weights[i][0] = (
            weights[i][...].astype(f32)
            - outer_rate * inner_rate * (average + momentum_decay * new_moment)
        ).astype(b16)


def update(grads, weights, moments, sharers):
    hidden, width = weights[1].shape
    steps = 4
    up = pl.BlockSpec((width // steps, hidden), lambda i: (i, 0))
    up_grad = pl.BlockSpec((hidden, width // steps), lambda i: (0, i))
    down = pl.BlockSpec((hidden // steps, width), lambda i: (i, 0))
    new_up = pl.BlockSpec((1, width // steps, hidden), lambda i: (0, i, 0))
    new_down = pl.BlockSpec((1, hidden // steps, width), lambda i: (0, i, 0))
    return pl.pallas_call(
        functools.partial(update_kernel, sharers),
        name="update",
        grid=(steps,),
        out_shape=[jax.ShapeDtypeStruct((1,) + w.shape, b16) for w in weights] * 2,
        in_specs=[up_grad, down] * 2 + [up, down, up, down] * 2,
        out_specs=[new_up, new_down, new_up, new_down] * 2,
        compiler_params=pltpu.CompilerParams(vmem_limit_bytes=60 * 2**20),
    )(*grads, *weights, *moments)


def gelu_and_slope(v):
    scale, cubic = 0.7978845608028654, 0.044715
    square = v * v
    t = jnp.tanh(scale * v * (1.0 + cubic * square))
    half = 0.5 * (1.0 + t)
    slope = half + 0.5 * v * (1.0 - t * t) * (scale * (1.0 + 3.0 * cubic * square))
    return v * half, slope


def dot(a, b):
    return jnp.dot(a, b, preferred_element_type=f32)


def dot_rows(a, b):
    return lax.dot_general(a, b, (((0,), (0,)), ((), ())), preferred_element_type=f32)


def dot_cols(a, b):
    return lax.dot_general(a, b, (((1,), (1,)), ((), ())), preferred_element_type=f32)


class Place:
    def __init__(self):
        row, col = lax.axis_index("row"), lax.axis_index("col")
        self.zl, self.x = row // 4, row % 4
        self.zh, self.y, self.k = col // 8, (col // 2) % 4, col % 2
        self.stay = (self.zl % 2) == self.k
        other_zl = self.zl + 1 - 2 * (self.zl % 2)
        self.swap = (other_zl * 4 + self.x, self.zh * 8 + self.y * 2 + (1 - self.k))


class ColGroup:
    def __init__(self, place):
        self.place = place
        self.p, self.t, self.k = place.zh, place.y, place.k

    def device(self, p, t, k):
        return (self.place.zl * 4 + self.place.x, p * 8 + t * 2 + k)


class RowGroup:
    def __init__(self, place):
        self.place = place
        self.p, self.t, self.k = place.zl // 2, place.x, place.k
        self.side = place.zl % 2

    def device(self, p, t, k):
        return ((p * 2 + self.side) * 4 + t, self.place.zh * 8 + self.place.y * 2 + k)


def slot(p, t, k):
    return k * 8 + p * 4 + t


def first_row(g, p, t, k):
    return pl.multiple_of((g * PATHS + slot(p, t, k)) * PART, PART)


def near(group):
    p, t, k = group.p, group.t, group.k
    up, down = (t + 1) % RING, (t + RING - 1) % RING
    return {
        "pair": group.device(1 - p, t, k),
        "sibling": group.device(p, t, 1 - k),
        "up": group.device(p, up, k),
        "down": group.device(p, down, k),
    }


def greet(devices):
    barrier = pltpu.get_barrier_semaphore()
    for device in devices:
        pl.semaphore_signal(barrier, inc=1, device_id=device, device_id_type=MESH)
    pl.semaphore_wait(barrier, len(devices))


class Mail:
    def __init__(self, send_sem, recv_sem):
        self.send_sem, self.recv_sem = send_sem, recv_sem
        self.sent = []
        self.used = 0
        self.notes = []

    def note(self, mark):
        self.notes.append(mark)

    def take(self, count):
        self.used += count
        return self.used - count

    def copy(self, number, src, dst, device):
        return pltpu.make_async_remote_copy(
            src_ref=src,
            dst_ref=dst,
            send_sem=self.send_sem.at[number],
            recv_sem=self.recv_sem.at[number],
            device_id=device,
            device_id_type=MESH,
        )

    def send(self, number, src, dst, device):
        copy = self.copy(number, src, dst, device)
        copy.start()
        self.sent.append(copy)

    def arrived(self, number, ref, device):
        self.copy(number, ref, ref, device).wait_recv()

    def finish(self):
        for copy in self.sent:
            copy.wait_send()
        self.sent = []


class Gather:
    def __init__(self, group, mail, region, half):
        self.g, self.mail, self.region, self.half = group, mail, region, half
        self.base = mail.take(17)
        self.peers = near(group)

    def send(self, m, ref, to):
        self.mail.send(self.base + m, ref, ref, self.peers[to])

    def numbers(self, *messages):
        return [self.base + m for m in messages]

    def got(self, m, ref):
        self.mail.arrived(self.base + m, ref, self.peers["sibling"])

    def steps(self):
        g = self.g
        p, t, k = g.p, g.t, g.k
        before, after, far = (t + RING - 1) % RING, (t + 1) % RING, (t + 2) % RING
        own = self.region(p, t, k)
        self.send(0, own, "pair")
        self.send(2, own, "up")
        self.send(3, own, "down")
        self.send(1, own, "sibling")
        yield self.numbers(2, 3)
        for q, first, fwd in ((p, 2, 7), (1 - p, 4, 11)):
            if first == 4:
                ref = self.region(q, t, k)
                self.got(0, ref)
                self.send(4, ref, "up")
                self.send(5, ref, "down")
                self.send(6, ref, "sibling")
                yield self.numbers(4, 5)
            ref = self.region(q, before, k)
            self.got(first, ref)
            self.send(fwd, self.half(q, before, k, 0), "up")
            self.send(fwd + 1, ref, "sibling")
            ref = self.region(q, after, k)
            self.got(first + 1, ref)
            self.send(fwd + 2, self.half(q, after, k, 1), "down")
            self.send(fwd + 3, ref, "sibling")
            yield self.numbers(0) if first == 2 else self.numbers(7, 9)
        for q, fwd, last in ((p, 7, 15), (1 - p, 11, 16)):
            self.got(fwd, self.half(q, far, k, 0))
            self.got(fwd + 2, self.half(q, far, k, 1))
            self.send(last, self.region(q, far, k), "sibling")
            yield self.numbers(11, 13) if last == 15 else self.numbers(1, 6, 8, 10, 12, 14, 15, 16)
        for m, q, s in (
            (1, p, t),
            (6, 1 - p, t),
            (8, p, before),
            (10, p, after),
            (12, 1 - p, before),
            (14, 1 - p, after),
            (15, p, far),
            (16, 1 - p, far),
        ):
            self.got(m, self.region(q, s, 1 - k))


def token_regions(buf, g):
    def region(p, t, k):
        return buf.at[pl.ds(first_row(g, p, t, k), PART)]

    def half(p, t, k, h):
        return buf.at[pl.ds(first_row(g, p, t, k) + h * (PART // 2), PART // 2)]

    return region, half


def add_rows(dst, at, left, left_at, right, right_at, count):
    step = 16

    def body(i, _):
        off = i * step
        dst[pl.ds(at + off, step)] = (
            left[pl.ds(left_at + off, step)].astype(f32)
            + right[pl.ds(right_at + off, step)].astype(f32)
        ).astype(b16)
        return 0

    lax.fori_loop(0, count // step, body, 0, unroll=2)


class Scatter:
    def __init__(self, group, mail, g, part, bufs, out):
        self.g, self.mail, self.n, self.part, self.out = group, mail, g, part, out
        self.base = mail.take(2 + 4 + 8 + 1)
        self.from_sibling, self.sums, self.from_far, self.from_near, self.from_pair = bufs
        self.peers = near(group)

    def steps(self):
        group, mail, part, n = self.g, self.mail, self.part, self.n
        from_sibling, sums, from_far, from_near, from_pair = (
            self.from_sibling.at[n],
            self.sums.at[n],
            self.from_far.at[n],
            self.from_near.at[n],
            self.from_pair.at[n],
        )
        p, t, k = group.p, group.t, group.k
        peers = self.peers
        half = PART // 2
        side = {1: 1 - p, 0: p}
        sib, far, nearby, pair = self.base, self.base + 2, self.base + 6, self.base + 14

        def cell(q, s):
            return pl.multiple_of((side[q] * 4 + (t + s) % RING) * PART, PART)

        def got(number, ref):
            mail.arrived(number, ref, peers["sibling"])

        for q in (1, 0):
            four = pl.ds(pl.multiple_of(side[q] * 4 * PART, 4 * PART), 4 * PART)
            src = part.at[pl.ds(first_row(n, side[q], 0, 1 - k), 4 * PART)]
            mail.send(sib + q, src, from_sibling.at[four], peers["sibling"])
        yield [sib + 1]

        def chip_sum(q, s):
            own = first_row(n, side[q], (t + s) % RING, k)
            add_rows(sums, cell(q, s), part, own, from_sibling, cell(q, s), PART)

        for q in (1, 0):
            if q == 0:
                yield [sib]
            four = pl.ds(pl.multiple_of(side[q] * 4 * PART, 4 * PART), 4 * PART)
            got(sib + q, from_sibling.at[four])
            chip_sum(q, 2)
            c = cell(q, 2)
            mail.send(far + 2 * q, sums.at[pl.ds(c, half)], from_far.at[2 * q], peers["up"])
            mail.send(
                far + 2 * q + 1, sums.at[pl.ds(c + half, half)], from_far.at[2 * q + 1], peers["down"]
            )
            chip_sum(q, 1)
            low = pl.ds(cell(q, 1) + half, half)
            mail.send(
                nearby + 4 * q, sums.at[low], from_near.at[2 * q, pl.ds(half, half)], peers["up"]
            )
            chip_sum(q, 3)
            top = pl.ds(cell(q, 3), half)
            mail.send(
                nearby + 4 * q + 1, sums.at[top], from_near.at[2 * q + 1, pl.ds(0, half)], peers["down"]
            )
        for q in (1, 0):
            chip_sum(q, 0)
        for q in (1, 0):
            yield [far + 2 * q, far + 2 * q + 1]
            got(far + 2 * q, from_far.at[2 * q])
            c = cell(q, 1)
            add_rows(sums, c, sums, c, from_far.at[2 * q], 0, half)
            mail.send(
                nearby + 4 * q + 2,
                sums.at[pl.ds(c, half)],
                from_near.at[2 * q, pl.ds(0, half)],
                peers["up"],
            )
            got(far + 2 * q + 1, from_far.at[2 * q + 1])
            c = pl.multiple_of(cell(q, 3) + half, half)
            add_rows(sums, c, sums, c, from_far.at[2 * q + 1], 0, half)
            mail.send(
                nearby + 4 * q + 3,
                sums.at[pl.ds(c, half)],
                from_near.at[2 * q + 1, pl.ds(half, half)],
                peers["down"],
            )

        def wait_near(q):
            got(nearby + 4 * q, from_near.at[2 * q, pl.ds(half, half)])
            got(nearby + 4 * q + 1, from_near.at[2 * q + 1, pl.ds(0, half)])
            got(nearby + 4 * q + 2, from_near.at[2 * q, pl.ds(0, half)])
            got(nearby + 4 * q + 3, from_near.at[2 * q + 1, pl.ds(half, half)])

        def total(q, i):
            rows = pl.ds(i * 16, 16)
            return (
                sums[pl.ds(cell(q, 0) + i * 16, 16)].astype(f32)
                + from_near[2 * q, rows].astype(f32)
                + from_near[2 * q + 1, rows].astype(f32)
            )

        yield [nearby + 4 + i for i in range(4)]
        wait_near(1)

        def pair_part(i, _):
            sums[pl.ds(cell(1, 0) + i * 16, 16)] = total(1, i).astype(b16)
            return 0

        lax.fori_loop(0, PART // 16, pair_part, 0)
        mail.send(pair, sums.at[pl.ds(cell(1, 0), PART)], from_pair, peers["pair"])
        yield [nearby + i for i in range(4)]
        wait_near(0)
        yield [pair]
        got(pair, from_pair)

        def own_part(i, _):
            rows = pl.ds(i * 16, 16)
            self.out[rows] = (total(0, i) + from_pair[rows].astype(f32)).astype(self.out.dtype)
            return 0

        lax.fori_loop(0, PART // 16, own_part, 0)


def scatter_scratch(width):
    return [
        pltpu.VMEM((GROUPS, 8 * PART, width), b16),
        pltpu.VMEM((GROUPS, 8 * PART, width), b16),
        pltpu.VMEM((GROUPS, 4, PART // 2, width), b16),
        pltpu.VMEM((GROUPS, 4, PART, width), b16),
        pltpu.VMEM((GROUPS, PART, width), b16),
    ]


class Swap:
    def __init__(self, place, mail):
        self.place, self.mail, self.number = place, mail, mail.take(1)

    def start(self, src, own_dst, swap_dst):
        self.src, self.dst = src, swap_dst

        @pl.when(self.place.stay)
        def _():
            own_dst[...] = src[...]

        @pl.when(jnp.logical_not(self.place.stay))
        def _():
            self.mail.copy(self.number, src, swap_dst, self.place.swap).start()

    def wait(self):
        @pl.when(jnp.logical_not(self.place.stay))
        def _():
            self.mail.copy(self.number, self.src, self.dst, self.place.swap).wait()


def whole_step(
    pieces, cot, up_one, down_one, up_two, down_two,
    grad_up_one, grad_down_one, grad_up_two, grad_down_two,
    wide, other, inputs, normed_one, slope_one, act_one, part_one,
    cots, up_home, down_home, mixed, middle, mine, normed_two, act_two, slope_two, part_two,
    sum_up_two, sum_down_two, ready_up_two, ready_down_two, back_mine, back, group,
    *scratch,
):
    col_bufs, row_bufs, (send_sem, recv_sem) = scratch[:5], scratch[5:10], scratch[10:]
    place = Place()
    col, row = ColGroup(place), RowGroup(place)
    mail = Mail(send_sem, recv_sem)
    peers_c, peers_r = near(col), near(row)
    greet(
        [peers_c["sibling"], peers_c["pair"], peers_c["up"], peers_c["down"]]
        + [peers_r["pair"], peers_r["up"], peers_r["down"], place.swap]
    )
    k = place.k
    half_rows = ROWS // 2
    my_row = functools.partial(first_row, p=row.p, t=row.t, k=row.k)
    swap_row = functools.partial(first_row, p=row.p, t=row.t, k=1 - row.k)

    def normal_factor(values):
        return lax.rsqrt(jnp.mean(values * values, axis=-1, keepdims=True) + epsilon)

    def rows_of(g, i):
        return pl.ds(pl.multiple_of(g * ROWS + i * CHUNK, CHUNK), CHUNK)

    def accumulate(ref, fresh, value):
        if fresh is True:
            ref[...] = value
        elif fresh is False:
            ref[...] += value

    def chunks(body):
        lax.fori_loop(0, ROWS // CHUNK, lambda i, c: (body(i), c)[1], 0)

    def level_one(g):
        def body(i):
            rows = rows_of(g, i)
            values = inputs[rows].astype(f32)
            normed = (values * normal_factor(values)).astype(b16)
            normed_one[rows] = normed
            act, slope = gelu_and_slope(dot(normed, up_one[...]))
            slope_one[rows] = slope
            act = act.astype(b16)
            act_one[rows] = act
            part_one[rows] = dot(act, down_one[...]).astype(b16)

        chunks(body)

    def level_two(g):
        def body(i):
            rows = rows_of(g, i)
            act, slope = gelu_and_slope(dot(normed_two[rows], up_home[...]))
            act_two[rows] = act.astype(b16)
            slope = (slope * dot_cols(cots[rows], down_home[...])).astype(b16)
            slope_two[rows] = slope
            part_two[rows] = dot_cols(slope, up_home[...]).astype(b16)

        chunks(body)

    def level_two_grads(g):
        def body(i):
            rows = rows_of(g, i)
            sum_down_two[...] += dot_rows(act_two[rows], cots[rows])
            sum_up_two[...] += dot_rows(slope_two[rows], normed_two[rows])

        chunks(body)

    def level_one_back(g):
        def body(i):
            rows = rows_of(g, i)
            upstream = group[rows]
            grad_down_one[...] += dot_rows(act_one[rows], upstream)
            slope = (slope_one[rows] * dot_cols(upstream, down_one[...])).astype(b16)
            grad_up_one[...] += dot_rows(slope, normed_one[rows])

        chunks(body)

    swaps = {name: Swap(place, mail) for name in ("up", "down", "grad_up", "grad_down")}

    def chain(g):
        number = mail.take(1)
        for path in range(PATHS):
            own = pieces[pl.ds(path * TOKENS + g * PART, PART)]
            to = g * ROWS + slot(path // 8, path // 2 % RING, path % 2) * PART
            wide[pl.ds(to, PART)] = jnp.concatenate([own, own], axis=1)
        there = pl.ds(pl.multiple_of(g * ROWS + (1 - k) * half_rows, half_rows), half_rows)
        here = pl.ds(pl.multiple_of(g * ROWS + k * half_rows, half_rows), half_rows)
        landed = other.at[pl.ds(g * half_rows, half_rows)]
        mail.send(number, wide.at[there], landed, peers_c["sibling"])
        yield [number]
        mail.arrived(number, landed, peers_c["sibling"])
        lane = lax.broadcasted_iota(jnp.int32, (half_rows, 128), 1) // 64

        def lanes(p, t):
            return pl.ds(pl.multiple_of((p * 4 + t) * 128, 128), 128)

        inputs[here, lanes(col.p, col.t)] = jnp.where(lane == k, wide[here], landed[...])

        def region(p, t, k):
            at = pl.multiple_of(g * ROWS + k * half_rows, half_rows)
            return inputs.at[pl.ds(at, half_rows), lanes(p, t)]

        def half(p, t, k, h):
            quarter = half_rows // 2
            at = pl.multiple_of(g * ROWS + k * half_rows + h * quarter, quarter)
            return inputs.at[pl.ds(at, quarter), lanes(p, t)]

        for step, awaited in enumerate(Gather(col, mail, region, half).steps()):
            if step == EARLY and g == GROUPS - 1:
                swaps["up"].start(up_two, up_home, up_home)
                swaps["down"].start(down_two, down_home, down_home)
            yield awaited
        level_one(g)
        yield from Scatter(col, mail, g, part_one, col_bufs, mixed).steps()
        own_input = inputs[pl.ds(first_row(g, col.p, col.t, col.k), PART)]
        values = own_input.astype(f32) + mixed[...]
        middle[g] = values
        mine[g] = (values * normal_factor(values)).astype(b16)
        swap = Swap(place, mail)
        swap.start(
            mine.at[g],
            normed_two.at[pl.ds(my_row(g), PART)],
            normed_two.at[pl.ds(swap_row(g), PART)],
        )
        yield [swap.number]
        swap.wait()
        yield from Gather(row, mail, *token_regions(normed_two, g)).steps()
        if -1 - g not in mail.notes:
            yield [-1 - g]
        assert -1 - g in mail.notes
        if g == 0:
            yield [swaps["up"].number, swaps["down"].number]
            swaps["up"].wait()
            swaps["down"].wait()
        level_two(g)
        scatter = Scatter(row, mail, g, part_two, row_bufs, back_mine.at[g]).steps()
        yield next(scatter)
        yield next(scatter)
        awaited = next(scatter)
        level_two_grads(g)
        yield awaited
        yield from scatter
        swap = Swap(place, mail)
        swap.start(back_mine.at[g], back.at[g], back.at[g])
        yield [swap.number]
        swap.wait()
        upstream = back[g].astype(f32)
        values = middle[g]
        factor = normal_factor(values)
        through = factor * upstream - values * (factor * factor * factor) * jnp.mean(
            upstream * values, axis=-1, keepdims=True
        )
        own_cot = cot[pl.ds(g * PART, PART)].astype(f32)
        group[pl.ds(first_row(g, col.p, col.t, col.k), PART)] = (own_cot + through).astype(b16)
        for step, awaited in enumerate(Gather(col, mail, *token_regions(group, g)).steps()):
            if step == LATE and g == GROUPS - 1:
                ready_up_two[...] = sum_up_two[...].astype(b16)
                ready_down_two[...] = sum_down_two[...].astype(b16)
                swaps["grad_up"].start(ready_up_two, grad_up_two, grad_up_two)
                swaps["grad_down"].start(ready_down_two, grad_down_two, grad_down_two)
            yield awaited
        level_one_back(g)

    def background():
        for ref in (grad_up_one, grad_down_one, sum_up_two, sum_down_two):
            ref[...] = jnp.zeros_like(ref)
        cot_swaps = [Swap(place, mail) for _ in range(GROUPS)]
        for g, swap in enumerate(cot_swaps):
            swap.start(
                cot.at[pl.ds(g * PART, PART)],
                cots.at[pl.ds(my_row(g), PART)],
                cots.at[pl.ds(swap_row(g), PART)],
            )
        yield [swap.number for swap in cot_swaps]
        for g, swap in enumerate(cot_swaps):
            swap.wait()
        for g in range(GROUPS):
            yield from Gather(row, mail, *token_regions(cots, g)).steps()
            mail.note(-1 - g)

    tasks = [chain(g) for g in range(GROUPS)] + [background()]
    for task in ORDER:
        next(tasks[int(task)], None)
    swaps["grad_up"].wait()
    swaps["grad_down"].wait()
    mail.finish()


def gradients(*args):
    vmem = pl.BlockSpec(memory_space=pltpu.VMEM)
    width, hidden = args[2].shape
    count = args[0].shape[0]
    out_shape = [jax.ShapeDtypeStruct((hidden, width), f32)] * 2
    out_shape += [jax.ShapeDtypeStruct((hidden, width), b16)] * 2
    tokens_b16 = pltpu.VMEM((count, width), b16)
    part_b16 = pltpu.VMEM((GROUPS, PART, width), b16)
    hidden_b16 = pltpu.VMEM((count, hidden), b16)
    grad_f32 = pltpu.VMEM((hidden, width), f32)
    grad_b16 = pltpu.VMEM((hidden, width), b16)
    scratch = [
        pltpu.VMEM((count, 128), b16),
        pltpu.VMEM((count // 2, 128), b16),
        tokens_b16,
        tokens_b16,
        pltpu.VMEM((count, hidden), f32),
        hidden_b16,
        tokens_b16,
        tokens_b16,
        pltpu.VMEM((width, hidden), b16),
        pltpu.VMEM((hidden, width), b16),
        pltpu.VMEM((PART, width), f32),
        pltpu.VMEM((GROUPS, PART, width), f32),
        part_b16,
        tokens_b16,
        hidden_b16,
        hidden_b16,
        tokens_b16,
        grad_f32,
        grad_f32,
        grad_b16,
        grad_b16,
        part_b16,
        part_b16,
        tokens_b16,
    ]
    scratch += scatter_scratch(width) + scatter_scratch(width)
    messages = GROUPS * (1 + 17 + 15 + 1 + 17 + 15 + 1 + 17 + 1 + 17) + 4
    scratch += [pltpu.SemaphoreType.DMA((messages,)), pltpu.SemaphoreType.DMA((messages,))]
    return pl.pallas_call(
        whole_step,
        name="whole_step",
        out_shape=out_shape,
        in_specs=[vmem] * len(args),
        out_specs=[vmem] * len(out_shape),
        scratch_shapes=scratch,
        compiler_params=pltpu.CompilerParams(
            collective_id=COLLECTIVE, has_side_effects=True, vmem_limit_bytes=60 * 2**20
        ),
    )(*args)


def on_device(
    token_ids,
    embedding,
    up_one,
    down_one,
    up_two,
    down_two,
    moment_up_one,
    moment_down_one,
    moment_up_two,
    moment_down_two,
    cotangent,
):
    sharers = PATHS
    ids = token_ids[0].reshape(-1)
    pieces = embedding.at[ids].get(mode="promise_in_bounds")
    grads = gradients(
        pieces, cotangent[0, 0], up_one[0], down_one[0], up_two[0], down_two[0]
    )
    return update(
        grads,
        (up_one[0], down_one[0], up_two[0], down_two[0]),
        (moment_up_one[0], moment_down_one[0], moment_up_two[0], moment_down_two[0]),
        sharers,
    )


def solution(mesh):
    in_specs = (
        P("row", None, None),
        P(None, "col"),
        P("row", None, "col"),
        P("row", "col", None),
        P("col", None, "row"),
        P("col", "row", None),
        P("row", None, "col"),
        P("row", "col", None),
        P("col", None, "row"),
        P("col", "row", None),
        P("row", "col", None, None),
    )
    out_specs = (
        P("row", None, "col"),
        P("row", "col", None),
        P("col", None, "row"),
        P("col", "row", None),
        P("row", None, "col"),
        P("row", "col", None),
        P("col", None, "row"),
        P("col", "row", None),
    )
    return jax.shard_map(
        on_device, mesh=mesh, in_specs=in_specs, out_specs=out_specs, check_vma=False
    )
```

```python
import functools

import jax
import jax.numpy as jnp
from jax import lax
from jax.experimental import pallas as pl
from jax.experimental.pallas import tpu as pltpu
from jax.sharding import PartitionSpec as P

epsilon = 1e-06
momentum_decay = 0.9
outer_rate = 0.7
inner_rate = 0.01
MESH = pl.DeviceIdType.MESH
RING = 4
PATHS = 16
TOKENS = 128
GROUPS = 2
PART = TOKENS // GROUPS
ROWS = PATHS * PART
ORDER = (
    0, 1, 0, 1, 2, 0, 0, 1, 0, 0, 1, 2, 0, 0, 1, 1, 2, 2, 0, 0, 1, 1, 0, 0, 2, 2, 1, 0, 1, 2,
    0, 2, 1, 1, 2, 0, 1, 1, 0, 2, 0, 1, 2, 2, 2, 1, 2, 0, 1, 0, 0, 1, 0, 0, 0, 1, 1, 0, 0, 1,
    1, 0, 0, 1, 1, 0, 0, 1, 1, 1, 1, 0, 0, 1, 0, 0, 1, 0, 0, 1, 1, 0, 0, 1, 1, 1, 1,
)
CHUNK = 256
COLLECTIVE = 0
LATE = 2
EARLY = 3
f32, b16 = jnp.float32, jnp.bfloat16


def update_kernel(sharers, *refs):
    grads, weights, moments, new_weights, new_moments = (refs[4 * i : 4 * i + 4] for i in range(5))
    for i in range(4):
        gradient = grads[i][...].astype(f32)
        if i % 2 == 0:
            gradient = gradient.T
        average = gradient * (1.0 / sharers)
        new_moment = momentum_decay * moments[i][...].astype(f32) + average
        new_moments[i][0] = new_moment.astype(b16)
        new_weights[i][0] = (
            weights[i][...].astype(f32)
            - outer_rate * inner_rate * (average + momentum_decay * new_moment)
        ).astype(b16)


def update(grads, weights, moments, sharers):
    hidden, width = weights[1].shape
    steps = 4
    up = pl.BlockSpec((width // steps, hidden), lambda i: (i, 0))
    up_grad = pl.BlockSpec((hidden, width // steps), lambda i: (0, i))
    down = pl.BlockSpec((hidden // steps, width), lambda i: (i, 0))
    new_up = pl.BlockSpec((1, width // steps, hidden), lambda i: (0, i, 0))
    new_down = pl.BlockSpec((1, hidden // steps, width), lambda i: (0, i, 0))
    return pl.pallas_call(
        functools.partial(update_kernel, sharers),
        name="update",
        grid=(steps,),
        out_shape=[jax.ShapeDtypeStruct((1,) + w.shape, b16) for w in weights] * 2,
        in_specs=[up_grad, down] * 2 + [up, down, up, down] * 2,
        out_specs=[new_up, new_down, new_up, new_down] * 2,
        compiler_params=pltpu.CompilerParams(vmem_limit_bytes=60 * 2**20),
    )(*grads, *weights, *moments)


def gelu_and_slope(v):
    scale, cubic = 0.7978845608028654, 0.044715
    square = v * v
    t = jnp.tanh(scale * v * (1.0 + cubic * square))
    half = 0.5 * (1.0 + t)
    slope = half + 0.5 * v * (1.0 - t * t) * (scale * (1.0 + 3.0 * cubic * square))
    return v * half, slope


def dot(a, b):
    return jnp.dot(a, b, preferred_element_type=f32)


def dot_rows(a, b):
    return lax.dot_general(a, b, (((0,), (0,)), ((), ())), preferred_element_type=f32)


def dot_cols(a, b):
    return lax.dot_general(a, b, (((1,), (1,)), ((), ())), preferred_element_type=f32)


class Place:
    def __init__(self):
        row, col = lax.axis_index("row"), lax.axis_index("col")
        self.zl, self.x = row // 4, row % 4
        self.zh, self.y, self.k = col // 8, (col // 2) % 4, col % 2
        self.stay = (self.zl % 2) == self.k
        other_zl = self.zl + 1 - 2 * (self.zl % 2)
        self.swap = (other_zl * 4 + self.x, self.zh * 8 + self.y * 2 + (1 - self.k))


class ColGroup:
    def __init__(self, place):
        self.place = place
        self.p, self.t, self.k = place.zh, place.y, place.k

    def device(self, p, t, k):
        return (self.place.zl * 4 + self.place.x, p * 8 + t * 2 + k)


class RowGroup:
    def __init__(self, place):
        self.place = place
        self.p, self.t, self.k = place.zl // 2, place.x, place.k
        self.side = place.zl % 2

    def device(self, p, t, k):
        return ((p * 2 + self.side) * 4 + t, self.place.zh * 8 + self.place.y * 2 + k)


def slot(p, t, k):
    return k * 8 + p * 4 + t


def first_row(g, p, t, k):
    return pl.multiple_of((g * PATHS + slot(p, t, k)) * PART, PART)


def near(group):
    p, t, k = group.p, group.t, group.k
    up, down = (t + 1) % RING, (t + RING - 1) % RING
    return {
        "pair": group.device(1 - p, t, k),
        "sibling": group.device(p, t, 1 - k),
        "up": group.device(p, up, k),
        "down": group.device(p, down, k),
    }


def greet(devices):
    barrier = pltpu.get_barrier_semaphore()
    for device in devices:
        pl.semaphore_signal(barrier, inc=1, device_id=device, device_id_type=MESH)
    pl.semaphore_wait(barrier, len(devices))


class Mail:
    def __init__(self, send_sem, recv_sem):
        self.send_sem, self.recv_sem = send_sem, recv_sem
        self.sent = []
        self.used = 0
        self.notes = []

    def note(self, mark):
        self.notes.append(mark)

    def take(self, count):
        self.used += count
        return self.used - count

    def copy(self, number, src, dst, device):
        return pltpu.make_async_remote_copy(
            src_ref=src,
            dst_ref=dst,
            send_sem=self.send_sem.at[number],
            recv_sem=self.recv_sem.at[number],
            device_id=device,
            device_id_type=MESH,
        )

    def send(self, number, src, dst, device):
        copy = self.copy(number, src, dst, device)
        copy.start()
        self.sent.append(copy)

    def arrived(self, number, ref, device):
        self.copy(number, ref, ref, device).wait_recv()

    def finish(self):
        for copy in self.sent:
            copy.wait_send()
        self.sent = []


class Gather:
    def __init__(self, group, mail, region, half):
        self.g, self.mail, self.region, self.half = group, mail, region, half
        self.base = mail.take(17)
        self.peers = near(group)

    def send(self, m, ref, to):
        self.mail.send(self.base + m, ref, ref, self.peers[to])

    def numbers(self, *messages):
        return [self.base + m for m in messages]

    def got(self, m, ref):
        self.mail.arrived(self.base + m, ref, self.peers["sibling"])

    def steps(self):
        g = self.g
        p, t, k = g.p, g.t, g.k
        before, after, far = (t + RING - 1) % RING, (t + 1) % RING, (t + 2) % RING
        own = self.region(p, t, k)
        self.send(0, own, "pair")
        self.send(2, own, "up")
        self.send(3, own, "down")
        self.send(1, own, "sibling")
        yield self.numbers(2, 3)
        for q, first, fwd in ((p, 2, 7), (1 - p, 4, 11)):
            if first == 4:
                ref = self.region(q, t, k)
                self.got(0, ref)
                self.send(4, ref, "up")
                self.send(5, ref, "down")
                self.send(6, ref, "sibling")
                yield self.numbers(4, 5)
            ref = self.region(q, before, k)
            self.got(first, ref)
            self.send(fwd, self.half(q, before, k, 0), "up")
            self.send(fwd + 1, ref, "sibling")
            ref = self.region(q, after, k)
            self.got(first + 1, ref)
            self.send(fwd + 2, self.half(q, after, k, 1), "down")
            self.send(fwd + 3, ref, "sibling")
            yield self.numbers(0) if first == 2 else self.numbers(7, 9)
        for q, fwd, last in ((p, 7, 15), (1 - p, 11, 16)):
            self.got(fwd, self.half(q, far, k, 0))
            self.got(fwd + 2, self.half(q, far, k, 1))
            self.send(last, self.region(q, far, k), "sibling")
            yield self.numbers(11, 13) if last == 15 else self.numbers(1, 6, 8, 10, 12, 14, 15, 16)
        for m, q, s in (
            (1, p, t),
            (6, 1 - p, t),
            (8, p, before),
            (10, p, after),
            (12, 1 - p, before),
            (14, 1 - p, after),
            (15, p, far),
            (16, 1 - p, far),
        ):
            self.got(m, self.region(q, s, 1 - k))


def token_regions(buf, g):
    def region(p, t, k):
        return buf.at[pl.ds(first_row(g, p, t, k), PART)]

    def half(p, t, k, h):
        return buf.at[pl.ds(first_row(g, p, t, k) + h * (PART // 2), PART // 2)]

    return region, half


def add_rows(dst, at, left, left_at, right, right_at, count):
    step = 16

    def body(i, _):
        off = i * step
        dst[pl.ds(at + off, step)] = (
            left[pl.ds(left_at + off, step)].astype(f32)
            + right[pl.ds(right_at + off, step)].astype(f32)
        ).astype(b16)
        return 0

    lax.fori_loop(0, count // step, body, 0, unroll=2)


class Scatter:
    def __init__(self, group, mail, g, part, bufs, out):
        self.g, self.mail, self.n, self.part, self.out = group, mail, g, part, out
        self.base = mail.take(2 + 4 + 8 + 1)
        self.from_sibling, self.sums, self.from_far, self.from_near, self.from_pair = bufs
        self.peers = near(group)

    def steps(self):
        group, mail, part, n = self.g, self.mail, self.part, self.n
        from_sibling, sums, from_far, from_near, from_pair = (
            self.from_sibling.at[n],
            self.sums.at[n],
            self.from_far.at[n],
            self.from_near.at[n],
            self.from_pair.at[n],
        )
        p, t, k = group.p, group.t, group.k
        peers = self.peers
        half = PART // 2
        side = {1: 1 - p, 0: p}
        sib, far, nearby, pair = self.base, self.base + 2, self.base + 6, self.base + 14

        def cell(q, s):
            return pl.multiple_of((side[q] * 4 + (t + s) % RING) * PART, PART)

        def got(number, ref):
            mail.arrived(number, ref, peers["sibling"])

        for q in (1, 0):
            four = pl.ds(pl.multiple_of(side[q] * 4 * PART, 4 * PART), 4 * PART)
            src = part.at[pl.ds(first_row(n, side[q], 0, 1 - k), 4 * PART)]
            mail.send(sib + q, src, from_sibling.at[four], peers["sibling"])
        yield [sib + 1]

        def chip_sum(q, s):
            own = first_row(n, side[q], (t + s) % RING, k)
            add_rows(sums, cell(q, s), part, own, from_sibling, cell(q, s), PART)

        for q in (1, 0):
            if q == 0:
                yield [sib]
            four = pl.ds(pl.multiple_of(side[q] * 4 * PART, 4 * PART), 4 * PART)
            got(sib + q, from_sibling.at[four])
            chip_sum(q, 2)
            c = cell(q, 2)
            mail.send(far + 2 * q, sums.at[pl.ds(c, half)], from_far.at[2 * q], peers["up"])
            mail.send(
                far + 2 * q + 1, sums.at[pl.ds(c + half, half)], from_far.at[2 * q + 1], peers["down"]
            )
            chip_sum(q, 1)
            low = pl.ds(cell(q, 1) + half, half)
            mail.send(
                nearby + 4 * q, sums.at[low], from_near.at[2 * q, pl.ds(half, half)], peers["up"]
            )
            chip_sum(q, 3)
            top = pl.ds(cell(q, 3), half)
            mail.send(
                nearby + 4 * q + 1, sums.at[top], from_near.at[2 * q + 1, pl.ds(0, half)], peers["down"]
            )
        for q in (1, 0):
            chip_sum(q, 0)
        for q in (1, 0):
            yield [far + 2 * q, far + 2 * q + 1]
            got(far + 2 * q, from_far.at[2 * q])
            c = cell(q, 1)
            add_rows(sums, c, sums, c, from_far.at[2 * q], 0, half)
            mail.send(
                nearby + 4 * q + 2,
                sums.at[pl.ds(c, half)],
                from_near.at[2 * q, pl.ds(0, half)],
                peers["up"],
            )
            got(far + 2 * q + 1, from_far.at[2 * q + 1])
            c = pl.multiple_of(cell(q, 3) + half, half)
            add_rows(sums, c, sums, c, from_far.at[2 * q + 1], 0, half)
            mail.send(
                nearby + 4 * q + 3,
                sums.at[pl.ds(c, half)],
                from_near.at[2 * q + 1, pl.ds(half, half)],
                peers["down"],
            )

        def wait_near(q):
            got(nearby + 4 * q, from_near.at[2 * q, pl.ds(half, half)])
            got(nearby + 4 * q + 1, from_near.at[2 * q + 1, pl.ds(0, half)])
            got(nearby + 4 * q + 2, from_near.at[2 * q, pl.ds(0, half)])
            got(nearby + 4 * q + 3, from_near.at[2 * q + 1, pl.ds(half, half)])

        def total(q, i):
            rows = pl.ds(i * 16, 16)
            return (
                sums[pl.ds(cell(q, 0) + i * 16, 16)].astype(f32)
                + from_near[2 * q, rows].astype(f32)
                + from_near[2 * q + 1, rows].astype(f32)
            )

        yield [nearby + 4 + i for i in range(4)]
        wait_near(1)

        def pair_part(i, _):
            sums[pl.ds(cell(1, 0) + i * 16, 16)] = total(1, i).astype(b16)
            return 0

        lax.fori_loop(0, PART // 16, pair_part, 0)
        mail.send(pair, sums.at[pl.ds(cell(1, 0), PART)], from_pair, peers["pair"])
        yield [nearby + i for i in range(4)]
        wait_near(0)
        yield [pair]
        got(pair, from_pair)

        def own_part(i, _):
            rows = pl.ds(i * 16, 16)
            self.out[rows] = (total(0, i) + from_pair[rows].astype(f32)).astype(self.out.dtype)
            return 0

        lax.fori_loop(0, PART // 16, own_part, 0)


def scatter_scratch(width):
    return [
        pltpu.VMEM((GROUPS, 8 * PART, width), b16),
        pltpu.VMEM((GROUPS, 8 * PART, width), b16),
        pltpu.VMEM((GROUPS, 4, PART // 2, width), b16),
        pltpu.VMEM((GROUPS, 4, PART, width), b16),
        pltpu.VMEM((GROUPS, PART, width), b16),
    ]


class Swap:
    def __init__(self, place, mail):
        self.place, self.mail, self.number = place, mail, mail.take(1)

    def start(self, src, own_dst, swap_dst):
        self.src, self.dst = src, swap_dst

        @pl.when(self.place.stay)
        def _():
            own_dst[...] = src[...]

        @pl.when(jnp.logical_not(self.place.stay))
        def _():
            self.mail.copy(self.number, src, swap_dst, self.place.swap).start()

    def wait(self):
        @pl.when(jnp.logical_not(self.place.stay))
        def _():
            self.mail.copy(self.number, self.src, self.dst, self.place.swap).wait()


def whole_step(
    pieces, cot, up_one, down_one, up_two, down_two,
    grad_up_one, grad_down_one, grad_up_two, grad_down_two,
    wide, other, inputs, normed_one, slope_one, act_one, part_one,
    cots, up_home, down_home, mixed, middle, mine, normed_two, act_two, slope_two, part_two,
    sum_up_two, sum_down_two, ready_up_two, ready_down_two, back_mine, back, group,
    *scratch,
):
    col_bufs, row_bufs, (send_sem, recv_sem) = scratch[:5], scratch[5:10], scratch[10:]
    place = Place()
    col, row = ColGroup(place), RowGroup(place)
    mail = Mail(send_sem, recv_sem)
    peers_c, peers_r = near(col), near(row)
    greet(
        [peers_c["sibling"], peers_c["pair"], peers_c["up"], peers_c["down"]]
        + [peers_r["pair"], peers_r["up"], peers_r["down"], place.swap]
    )
    k = place.k
    half_rows = ROWS // 2
    my_row = functools.partial(first_row, p=row.p, t=row.t, k=row.k)
    swap_row = functools.partial(first_row, p=row.p, t=row.t, k=1 - row.k)

    def normal_factor(values):
        return lax.rsqrt(jnp.mean(values * values, axis=-1, keepdims=True) + epsilon)

    def rows_of(g, i):
        return pl.ds(pl.multiple_of(g * ROWS + i * CHUNK, CHUNK), CHUNK)

    def accumulate(ref, fresh, value):
        if fresh is True:
            ref[...] = value
        elif fresh is False:
            ref[...] += value

    def chunks(body):
        lax.fori_loop(0, ROWS // CHUNK, lambda i, c: (body(i), c)[1], 0)

    def level_one(g):
        def body(i):
            rows = rows_of(g, i)
            values = inputs[rows].astype(f32)
            normed = (values * normal_factor(values)).astype(b16)
            normed_one[rows] = normed
            act, slope = gelu_and_slope(dot(normed, up_one[...]))
            slope_one[rows] = slope
            act = act.astype(b16)
            act_one[rows] = act
            part_one[rows] = dot(act, down_one[...]).astype(b16)

        chunks(body)

    def level_two(g):
        def body(i):
            rows = rows_of(g, i)
            act, slope = gelu_and_slope(dot(normed_two[rows], up_home[...]))
            act_two[rows] = act.astype(b16)
            slope = (slope * dot_cols(cots[rows], down_home[...])).astype(b16)
            slope_two[rows] = slope
            part_two[rows] = dot_cols(slope, up_home[...]).astype(b16)

        chunks(body)

    def level_two_grads(g):
        def body(i):
            rows = rows_of(g, i)
            sum_down_two[...] += dot_rows(act_two[rows], cots[rows])
            sum_up_two[...] += dot_rows(slope_two[rows], normed_two[rows])

        chunks(body)

    def level_one_back(g):
        def body(i):
            rows = rows_of(g, i)
            upstream = group[rows]
            grad_down_one[...] += dot_rows(act_one[rows], upstream)
            slope = (slope_one[rows] * dot_cols(upstream, down_one[...])).astype(b16)
            grad_up_one[...] += dot_rows(slope, normed_one[rows])

        chunks(body)

    swaps = {name: Swap(place, mail) for name in ("up", "down", "grad_up", "grad_down")}

    def chain(g):
        number = mail.take(1)
        for path in range(PATHS):
            own = pieces[pl.ds(path * TOKENS + g * PART, PART)]
            to = g * ROWS + slot(path // 8, path // 2 % RING, path % 2) * PART
            wide[pl.ds(to, PART)] = jnp.concatenate([own, own], axis=1)
        there = pl.ds(pl.multiple_of(g * ROWS + (1 - k) * half_rows, half_rows), half_rows)
        here = pl.ds(pl.multiple_of(g * ROWS + k * half_rows, half_rows), half_rows)
        landed = other.at[pl.ds(g * half_rows, half_rows)]
        mail.send(number, wide.at[there], landed, peers_c["sibling"])
        yield [number]
        mail.arrived(number, landed, peers_c["sibling"])
        lane = lax.broadcasted_iota(jnp.int32, (half_rows, 128), 1) // 64

        def lanes(p, t):
            return pl.ds(pl.multiple_of((p * 4 + t) * 128, 128), 128)

        inputs[here, lanes(col.p, col.t)] = jnp.where(lane == k, wide[here], landed[...])

        def region(p, t, k):
            at = pl.multiple_of(g * ROWS + k * half_rows, half_rows)
            return inputs.at[pl.ds(at, half_rows), lanes(p, t)]

        def half(p, t, k, h):
            quarter = half_rows // 2
            at = pl.multiple_of(g * ROWS + k * half_rows + h * quarter, quarter)
            return inputs.at[pl.ds(at, quarter), lanes(p, t)]

        for step, awaited in enumerate(Gather(col, mail, region, half).steps()):
            if step == EARLY and g == GROUPS - 1:
                swaps["up"].start(up_two, up_home, up_home)
                swaps["down"].start(down_two, down_home, down_home)
            yield awaited
        level_one(g)
        yield from Scatter(col, mail, g, part_one, col_bufs, mixed).steps()
        own_input = inputs[pl.ds(first_row(g, col.p, col.t, col.k), PART)]
        values = own_input.astype(f32) + mixed[...]
        middle[g] = values
        mine[g] = (values * normal_factor(values)).astype(b16)
        swap = Swap(place, mail)
        swap.start(
            mine.at[g],
            normed_two.at[pl.ds(my_row(g), PART)],
            normed_two.at[pl.ds(swap_row(g), PART)],
        )
        yield [swap.number]
        swap.wait()
        yield from Gather(row, mail, *token_regions(normed_two, g)).steps()
        if -1 - g not in mail.notes:
            yield [-1 - g]
        assert -1 - g in mail.notes
        if g == 0:
            yield [swaps["up"].number, swaps["down"].number]
            swaps["up"].wait()
            swaps["down"].wait()
        level_two(g)
        scatter = Scatter(row, mail, g, part_two, row_bufs, back_mine.at[g]).steps()
        yield next(scatter)
        yield next(scatter)
        awaited = next(scatter)
        level_two_grads(g)
        yield awaited
        yield from scatter
        swap = Swap(place, mail)
        swap.start(back_mine.at[g], back.at[g], back.at[g])
        yield [swap.number]
        swap.wait()
        upstream = back[g].astype(f32)
        values = middle[g]
        factor = normal_factor(values)
        through = factor * upstream - values * (factor * factor * factor) * jnp.mean(
            upstream * values, axis=-1, keepdims=True
        )
        own_cot = cot[pl.ds(g * PART, PART)].astype(f32)
        group[pl.ds(first_row(g, col.p, col.t, col.k), PART)] = (own_cot + through).astype(b16)
        for step, awaited in enumerate(Gather(col, mail, *token_regions(group, g)).steps()):
            if step == LATE and g == GROUPS - 1:
                ready_up_two[...] = sum_up_two[...].astype(b16)
                ready_down_two[...] = sum_down_two[...].astype(b16)
                swaps["grad_up"].start(ready_up_two, grad_up_two, grad_up_two)
                swaps["grad_down"].start(ready_down_two, grad_down_two, grad_down_two)
            yield awaited
        level_one_back(g)

    def background():
        for ref in (grad_up_one, grad_down_one, sum_up_two, sum_down_two):
            ref[...] = jnp.zeros_like(ref)
        cot_swaps = [Swap(place, mail) for _ in range(GROUPS)]
        for g, swap in enumerate(cot_swaps):
            swap.start(
                cot.at[pl.ds(g * PART, PART)],
                cots.at[pl.ds(my_row(g), PART)],
                cots.at[pl.ds(swap_row(g), PART)],
            )
        yield [swap.number for swap in cot_swaps]
        for g, swap in enumerate(cot_swaps):
            swap.wait()
        for g in range(GROUPS):
            yield from Gather(row, mail, *token_regions(cots, g)).steps()
            mail.note(-1 - g)

    tasks = [chain(g) for g in range(GROUPS)] + [background()]
    for task in ORDER:
        next(tasks[int(task)], None)
    swaps["grad_up"].wait()
    swaps["grad_down"].wait()
    mail.finish()


def gradients(*args):
    vmem = pl.BlockSpec(memory_space=pltpu.VMEM)
    width, hidden = args[2].shape
    count = args[0].shape[0]
    out_shape = [jax.ShapeDtypeStruct((hidden, width), f32)] * 2
    out_shape += [jax.ShapeDtypeStruct((hidden, width), b16)] * 2
    tokens_b16 = pltpu.VMEM((count, width), b16)
    part_b16 = pltpu.VMEM((GROUPS, PART, width), b16)
    hidden_b16 = pltpu.VMEM((count, hidden), b16)
    grad_f32 = pltpu.VMEM((hidden, width), f32)
    grad_b16 = pltpu.VMEM((hidden, width), b16)
    scratch = [
        pltpu.VMEM((count, 128), b16),
        pltpu.VMEM((count // 2, 128), b16),
        tokens_b16,
        tokens_b16,
        pltpu.VMEM((count, hidden), f32),
        hidden_b16,
        tokens_b16,
        tokens_b16,
        pltpu.VMEM((width, hidden), b16),
        pltpu.VMEM((hidden, width), b16),
        pltpu.VMEM((PART, width), f32),
        pltpu.VMEM((GROUPS, PART, width), f32),
        part_b16,
        tokens_b16,
        hidden_b16,
        hidden_b16,
        tokens_b16,
        grad_f32,
        grad_f32,
        grad_b16,
        grad_b16,
        part_b16,
        part_b16,
        tokens_b16,
    ]
    scratch += scatter_scratch(width) + scatter_scratch(width)
    messages = GROUPS * (1 + 17 + 15 + 1 + 17 + 15 + 1 + 17 + 1 + 17) + 4
    scratch += [pltpu.SemaphoreType.DMA((messages,)), pltpu.SemaphoreType.DMA((messages,))]
    return pl.pallas_call(
        whole_step,
        name="whole_step",
        out_shape=out_shape,
        in_specs=[vmem] * len(args),
        out_specs=[vmem] * len(out_shape),
        scratch_shapes=scratch,
        compiler_params=pltpu.CompilerParams(
            collective_id=COLLECTIVE, has_side_effects=True, vmem_limit_bytes=60 * 2**20
        ),
    )(*args)


def on_device(
    token_ids,
    embedding,
    up_one,
    down_one,
    up_two,
    down_two,
    moment_up_one,
    moment_down_one,
    moment_up_two,
    moment_down_two,
    cotangent,
):
    sharers = PATHS
    ids = token_ids[0].reshape(-1)
    pieces = embedding.at[ids].get(mode="promise_in_bounds")
    grads = gradients(
        pieces, cotangent[0, 0], up_one[0], down_one[0], up_two[0], down_two[0]
    )
    return update(
        grads,
        (up_one[0], down_one[0], up_two[0], down_two[0]),
        (moment_up_one[0], moment_down_one[0], moment_up_two[0], moment_down_two[0]),
        sharers,
    )


def solution(mesh):
    in_specs = (
        P("row", None, None),
        P(None, "col"),
        P("row", None, "col"),
        P("row", "col", None),
        P("col", None, "row"),
        P("col", "row", None),
        P("row", None, "col"),
        P("row", "col", None),
        P("col", None, "row"),
        P("col", "row", None),
        P("row", "col", None, None),
    )
    out_specs = (
        P("row", None, "col"),
        P("row", "col", None),
        P("col", None, "row"),
        P("col", "row", None),
        P("row", None, "col"),
        P("row", "col", None),
        P("col", None, "row"),
        P("col", "row", None),
    )
    return jax.shard_map(
        on_device, mesh=mesh, in_specs=in_specs, out_specs=out_specs, check_vma=False
    )
```
